32 devices in a mesh: ctx: 8 (over z, y), fsdp: 4 (over x, core).
Axes of the slice: x: 2, y: 2, z: 4, core: 2. Of those that a mesh axis runs over, the one named last changes fastest.
Arguments:
- tokens: float32 [8, 2048, 768], P('fsdp', 'ctx'), may hold values from -6 to 6
- lengths: int32 [8], P('fsdp'), may hold values from 1 to 2048, as said below
- attend_weight: bfloat16 [768, 2304], P('fsdp'), may hold values from -0.21875 to 0.21875
- query_bias: bfloat16 [768], P('fsdp'), may hold values from -3 to 3
- value_bias: bfloat16 [768], P('fsdp'), may hold values from -3 to 3
- mixing_weight: bfloat16 [768, 768], P('fsdp'), may hold values from -6 to 6
- mixing_bias: bfloat16 [768], P('fsdp'), may hold values from -3 to 3
- first_gain: bfloat16 [768], P('fsdp'), may hold values from 0.25 to 1.75
- first_shift: bfloat16 [768], P('fsdp'), may hold values from -3 to 3
- up_weight: bfloat16 [768, 3072], P('fsdp'), may hold values from -0.21875 to 0.21875
- up_bias: bfloat16 [3072], P('fsdp'), may hold values from -3 to 3
- down_weight: bfloat16 [3072, 768], P('fsdp'), may hold values from -0.109375 to 0.109375
- down_bias: bfloat16 [768], P('fsdp'), may hold values from -3 to 3
- second_gain: bfloat16 [768], P('fsdp'), may hold values from 0.25 to 1.75
- second_shift: bfloat16 [768], P('fsdp'), may hold values from -3 to 3
- cotangent: float32 [8, 2048, 768], P('fsdp', 'ctx'), may hold values from -6 to 6
Outputs:
- result: float32 [8, 2048, 768], P('fsdp', 'ctx')
- tokens_grad: float32 [8, 2048, 768], P('fsdp', 'ctx')
- attend_grad: float32 [768, 2304], P('fsdp')
- querybias_grad: float32 [768], P('fsdp')
- valuebias_grad: float32 [768], P('fsdp')
- mixing_grad: float32 [768, 768], P('fsdp')
- mixingbias_grad: float32 [768], P('fsdp')
- firstgain_grad: float32 [768], P('fsdp')
- firstshift_grad: float32 [768], P('fsdp')
- upweight_grad: float32 [768, 3072], P('fsdp')
- upbias_grad: float32 [3072], P('fsdp')
- downweight_grad: float32 [3072, 768], P('fsdp')
- downbias_grad: float32 [768], P('fsdp')
- secondgain_grad: float32 [768], P('fsdp')
- secondshift_grad: float32 [768], P('fsdp')
The draws below stay inside these ranges and needn't reach their ends.
Inputs may be any that keep to these rules, and one draw needn't show every extreme that they name: `lengths`: each entry counts the real tokens of a sequence; positions at or past it are padding. Among the 2 sequences held by each index of fsdp, one chosen by the seed has exactly 2048.
All inputs are finite; a program needn't handle non-finite values.
Results may differ from the reference program's by a relative error of at most 0.022.
Values may be sent and summed in bfloat16 or wider, within the bound.
No kernel may reach another device: no remote copies, remote signals or barrier semaphores. Data moves between devices by JAX's collectives and lax.ppermute only.
A program may use at most 128 MiB of HBM per device.

```python
import math
import jax
import jax.numpy as jnp
from jax import lax

D = 768
F = 3072
HEAD_DIM = 64
SEQS = 2
LEN = 2048
NSEQ = 8


def draw_lengths(key, part):
    key = jax.random.fold_in(key, 7)
    base = jax.random.randint(jax.random.fold_in(key, 1), (NSEQ,), 1, LEN + 1)
    chosen = jax.random.randint(jax.random.fold_in(key, 2), (NSEQ // SEQS,), 0, SEQS)
    index = jnp.arange(NSEQ, dtype=jnp.int32)
    full = index % SEQS == jnp.repeat(chosen, SEQS)
    return jnp.where(full, LEN, base).astype(jnp.int32)


def block_scale(own_key, extent, pieces, low, high):
    def one(position, blocks):
        steps = jax.random.uniform(jax.random.fold_in(jax.random.fold_in(own_key, 6), position), (blocks,), jnp.float32, low / len(pieces), high / len(pieces))
        return jnp.repeat(jnp.exp(steps), extent[position] // blocks).reshape((-1,) + (1,) * (len(extent) - position - 1))

    loudness = one(*pieces[0])
    for cut in pieces[1:]:
        loudness = loudness * one(*cut)
    return loudness


def normal_values(key, extent, scale, most, pieces=(), held_as=jnp.bfloat16):
    level = block_scale(key, extent, pieces, -0.22, 0.18) if pieces else 1.0
    drawn = jax.random.normal(key, extent, jnp.float32) * scale * level
    return jnp.minimum(jnp.maximum(drawn, -most), most).astype(held_as)


def setup_inputs(seed: int = 0) -> dict:
    arg_keys = jax.random.split(jax.random.key(seed), 17)
    return {
        "tokens": normal_values(arg_keys[0], (NSEQ, LEN, D), 1.0, 6.0, ((0, 4), (1, 8)), jnp.float32),
        "lengths": draw_lengths(jax.random.fold_in(arg_keys[16], 71), 0),
        "attend_weight": normal_values(arg_keys[2], (D, 3 * D), D ** -0.5, 0.21875, ((0, 4),)),
        "query_bias": normal_values(arg_keys[3], (D,), 0.5, 3.0, ((0, 4),)),
        "value_bias": normal_values(arg_keys[4], (D,), 0.5, 3.0, ((0, 4),)),
        "mixing_weight": normal_values(arg_keys[5], (D, D), (max(1, 4 * D // LEN)) ** -0.5, 6.0, ((0, 4),)),
        "mixing_bias": normal_values(arg_keys[6], (D,), 0.5, 3.0, ((0, 4),)),
        "first_gain": jnp.clip(1.0 + 0.15 * jax.random.normal(arg_keys[7], (D,), jnp.float32), 0.25, 1.75).astype(jnp.bfloat16),
        "first_shift": normal_values(arg_keys[8], (D,), 0.5, 3.0, ((0, 4),)),
        "up_weight": normal_values(arg_keys[9], (D, F), D ** -0.5, 0.21875, ((0, 4),)),
        "up_bias": normal_values(arg_keys[10], (F,), 0.5, 3.0, ((0, 4),)),
        "down_weight": normal_values(arg_keys[11], (F, D), F ** -0.5, 0.109375, ((0, 4),)),
        "down_bias": normal_values(arg_keys[12], (D,), 0.5, 3.0, ((0, 4),)),
        "second_gain": jnp.clip(1.0 + 0.15 * jax.random.normal(arg_keys[13], (D,), jnp.float32), 0.25, 1.75).astype(jnp.bfloat16),
        "second_shift": normal_values(arg_keys[14], (D,), 0.5, 3.0, ((0, 4),)),
        "cotangent": normal_values(arg_keys[15], (NSEQ, LEN, D), 1.0, 6.0, ((0, 4), (1, 8)), jnp.float32),
    }


LN_TWO = math.log(2.0)
EPS = 1e-12
SCALE = 0.125
MASKED = -1e+30
HIGH = lax.Precision.HIGHEST

@jax.custom_vjp
def low(v):
    return lax.optimization_barrier(v.astype(jnp.bfloat16)).astype(jnp.float32)

@jax.custom_vjp
def low_back(v):
    return v

def low_keep(v):
    return (low(v), None)

def low_pass(kept, grad):
    return (grad,)

def back_keep(v):
    return (v, None)

def back_low(kept, grad):
    return (low(grad),)
low.defvjp(low_keep, low_pass)
low_back.defvjp(back_keep, back_low)

def layer_norm(value, gain, shift):
    mean = lax.optimization_barrier(jnp.mean(value, axis=-1, keepdims=True))
    centred = value - mean
    spread = lax.optimization_barrier(jnp.mean(centred * centred, axis=-1, keepdims=True))
    return centred * lax.rsqrt(spread + EPS) * gain + shift

def attention_block(query, keys, values, live):
    raw = jnp.einsum('qhd,khd->hqk', query, keys, precision=HIGH) * SCALE
    scores = low_back(jnp.where(live[None, None, :], raw, MASKED))
    level = LN_TWO * jnp.ceil(lax.optimization_barrier(jnp.max(scores, axis=-1, keepdims=True)) / LN_TWO)
    weights = jnp.exp(scores - level)
    total = lax.optimization_barrier(jnp.sum(weights, axis=-1))
    numer = low_back(jnp.einsum('hqk,khd->qhd', low(weights), values, precision=HIGH))
    return numer / jnp.transpose(total)[:, :, None]

def sequence_forward(tokens, live, params):
    attend, qbias, vbias, mixing, mixbias, fgain, fshift, upmat, upbias, downmat, downbias, sgain, sshift = params
    length, width = tokens.shape
    heads = width // HEAD_DIM
    projected = jnp.dot(low(tokens), attend, precision=HIGH)
    query = low(low_back(projected[:, :width] + qbias))
    keys = low(low_back(projected[:, width:2 * width]))
    values = low(low_back(projected[:, 2 * width:] + vbias))
    qsize = math.gcd(length, 512)
    query4 = query.reshape(length // qsize, qsize, heads, HEAD_DIM)
    keys3 = keys.reshape(length, heads, HEAD_DIM)
    values3 = values.reshape(length, heads, HEAD_DIM)

    def one_block(qblock):
        return attention_block(qblock, keys3, values3, live)
    attended = lax.map(jax.checkpoint(one_block), query4).reshape(length, width)
    mixed = low_back(jnp.dot(low(attended), mixing, precision=HIGH) + mixbias)
    first = layer_norm(tokens + mixed, fgain, fshift)
    pre = low_back(jnp.dot(low(first), upmat, precision=HIGH) + upbias)
    act = jax.nn.gelu(pre, approximate=False)
    branch = low_back(jnp.dot(low(act), downmat, precision=HIGH) + downbias)
    return layer_norm(first + branch, sgain, sshift)

def reference(tokens, lengths, attend_weight, query_bias, value_bias, mixing_weight, mixing_bias, first_gain, first_shift, up_weight, up_bias, down_weight, down_bias, second_gain, second_shift, cotangent):
    params = tuple((p.astype(jnp.float32) for p in (attend_weight, query_bias, value_bias, mixing_weight, mixing_bias, first_gain, first_shift, up_weight, up_bias, down_weight, down_bias, second_gain, second_shift)))

    def one_sequence(sums, item):
        seq_tokens, seq_length, seq_cot = item
        live = jnp.arange(LEN, dtype=jnp.int32) < seq_length

        def apply(values_in, params_in):
            return sequence_forward(values_in, live, params_in)
        output, backward = jax.vjp(apply, seq_tokens, params)
        token_grad, param_grad = backward(seq_cot)
        sums = jax.tree.map(lambda left, right: left + right, sums, param_grad)
        return (sums, (output, token_grad))
    zeros = jax.tree.map(jnp.zeros_like, params)
    sums, (outputs, grads) = lax.scan(one_sequence, zeros, (tokens, lengths, cotangent))
    return (outputs, grads, sums[0], sums[1], sums[2], sums[3], sums[4], sums[5], sums[6], sums[7], sums[8], sums[9], sums[10], sums[11], sums[12])
```

```python
import functools
import math

import jax
import jax.numpy as jnp
from jax import lax
from jax.experimental import pallas as pl
from jax.experimental.pallas import tpu as pltpu
from jax.sharding import PartitionSpec as P

HEAD_DIM = 64
LANES = 128
EPS = 1e-12
SCALE = 0.125
LOG2E = math.log2(math.e)
COEF = SCALE * LOG2E
MASKED = -1e30
SAFE = 60.0
MASK_LANE = 127
CORR_LANE = 36
VMEM = 48 * 1024 * 1024

f32 = jnp.float32
b16 = jnp.bfloat16


def xor_pairs(count, bit):
    return [(i, i ^ bit) for i in range(count)]


def ring_order(count):
    half = count // 2
    return [2 * p if p < half else 2 * (count - 1 - p) + 1 for p in range(count)]


def ring_slots(axis):
    count = lax.axis_size(axis)
    order = jnp.asarray(ring_order(count), jnp.int32)
    place = lax.axis_index(axis)
    spot = jnp.where(place % 2 == 0, place // 2, count - 1 - place // 2)
    steps = [0]
    for s in range(1, count // 2):
        steps += [-s, s]
    steps.append(count // 2)
    return order[jnp.mod(spot + jnp.asarray(steps, jnp.int32), count)]


def ring_gather(x, axis):
    count = lax.axis_size(axis)
    order = ring_order(count)
    right = [(order[p], order[(p + 1) % count]) for p in range(count)]
    left = [(d, s) for s, d in right]
    slots = [x]
    r = l = x
    for _ in range(1, count // 2):
        r = lax.ppermute(r, axis, right)
        l = lax.ppermute(l, axis, left)
        slots += [r, l]
    slots.append(
        jnp.concatenate(
            [lax.ppermute(r[:1], axis, right), lax.ppermute(l[1:], axis, left)], axis=0
        )
    )
    return slots


def bits_of(count):
    return [1 << k for k in range(count.bit_length() - 1)]


def gather_rows(w, axis):
    count = lax.axis_size(axis)
    i = lax.axis_index(axis)
    cur = w[None]
    for bit in bits_of(count)[1:]:
        other = lax.ppermute(cur, axis, xor_pairs(count, bit))
        low = (i // bit) % 2 == 0
        cur = jnp.concatenate([jnp.where(low, cur, other), jnp.where(low, other, cur)], 0)
    other = lax.ppermute(cur, axis, xor_pairs(count, 1))
    low = i % 2 == 0
    cur = jnp.stack([jnp.where(low, cur, other), jnp.where(low, other, cur)], 1)
    return cur.reshape((-1,) + w.shape[1:])


def halve(x, axis, bit):
    count = lax.axis_size(axis)
    upper = (lax.axis_index(axis) // bit) % 2
    half = x.shape[0] // 2
    send = lax.dynamic_slice_in_dim(x, (1 - upper) * half, half, 0)
    keep = lax.dynamic_slice_in_dim(x, upper * half, half, 0)
    got = lax.ppermute(send, axis, xor_pairs(count, bit))
    return (keep.astype(f32) + got.astype(f32)).astype(b16)


def unhalve(x, axis, bit):
    count = lax.axis_size(axis)
    low = (lax.axis_index(axis) // bit) % 2 == 0
    other = lax.ppermute(x, axis, xor_pairs(count, bit))
    return jnp.concatenate([jnp.where(low, x, other), jnp.where(low, other, x)], 0)


def reduce_rows(g):
    owners = lax.axis_size("fsdp")
    blocks = lax.axis_size("ctx")
    width = g.shape[-1]
    x = g.reshape(owners // 2, 2, -1, width).swapaxes(0, 1).reshape(g.shape)
    for bit in [1] + bits_of(owners)[1:][::-1]:
        x = halve(x, "fsdp", bit)
    if x.shape[0] % (8 * blocks):
        return lax.psum(x, "ctx").astype(f32)
    first = bits_of(blocks)
    second = [first[1], first[0]] + first[2:]
    half = width // 2
    a, b = x[:, :half], x[:, half:]
    for ba, bb in zip(first, second):
        a, b = halve(a, "ctx", ba), halve(b, "ctx", bb)
    for ba, bb in zip(first[::-1], second[::-1]):
        a, b = unhalve(a, "ctx", ba), unhalve(b, "ctx", bb)
    return jnp.concatenate([a, b], 1).astype(f32)


def dot_nt(a, b):
    return lax.dot_general(a, b, (((1,), (1,)), ((), ())), preferred_element_type=f32)


def dot_nn(a, b):
    return lax.dot_general(a, b, (((1,), (0,)), ((), ())), preferred_element_type=f32)


def lane_iota(rows):
    return lax.broadcasted_iota(jnp.int32, (rows, LANES), 1)


def split3(x):
    hi = x.astype(b16)
    rest = x - hi.astype(f32)
    mid = rest.astype(b16)
    low = (rest - mid.astype(f32)).astype(b16)
    return hi, mid, low


def place3(x, lane, at):
    hi, mid, low = (p.astype(f32) for p in split3(x))
    zero = jnp.zeros_like(x)
    return jnp.where(
        lane == at, hi, jnp.where(lane == at + 1, mid, jnp.where(lane == at + 2, low, zero))
    )


def stack_heads(pair):
    rows = pair.shape[0]
    lane = lane_iota(rows)
    zero = jnp.zeros_like(pair)
    return jnp.concatenate(
        [jnp.where(lane < HEAD_DIM, pair, zero), jnp.where(lane >= HEAD_DIM, pair, zero)], 0
    )


def join_heads(x):
    rows = x.shape[0] // 2
    return jnp.where(lane_iota(rows) < HEAD_DIM, x[:rows], x[rows:])


def key_extra(rows, base, length):
    lane = lane_iota(rows)
    dead = base + lax.broadcasted_iota(jnp.int32, (rows, LANES), 0) >= length
    mask = jnp.where(dead, MASKED, 0.0)
    return jnp.where(lane == MASK_LANE, mask, -1.0).astype(b16)


def forward_kernel(slots, bases, lengths, safe, q_ref, *refs):
    k_refs, v_refs = refs[:slots], refs[slots : 2 * slots]
    out_ref, extra_ref, level_ref = refs[2 * slots :]
    seq, pair = pl.program_id(0), pl.program_id(1)
    length = lengths[seq]
    rows = q_ref.shape[1]
    block = k_refs[0].shape[1]
    lane2 = lane_iota(2 * rows)
    stacked = stack_heads(q_ref[0])
    onehot = jnp.where(lane2 == MASK_LANE, 1.0, 0.0)
    level_ref[...] = jnp.zeros_like(level_ref)

    @pl.when(safe[seq * pl.num_programs(1) + pair] == 0)
    def _():
        top = jnp.full((2 * rows, 1), MASKED, f32)
        probe = jnp.concatenate([stacked, onehot.astype(b16)], 1)
        for s in range(slots):
            extra = key_extra(block, bases[s], length)
            scores = dot_nt(probe, jnp.concatenate([k_refs[s][0], extra], 1))
            top = jnp.maximum(top, jnp.max(scores, axis=1, keepdims=True))
        level_ref[...] = jnp.broadcast_to(jnp.ceil(top * COEF), level_ref.shape)

    level = level_ref[...]
    query = jnp.concatenate([stacked, (place3(level / COEF, lane2, 0) + onehot).astype(b16)], 1)
    ones = jnp.ones((block, LANES), b16)
    total = jnp.zeros((2 * rows, 2 * LANES), f32)
    for s in range(slots):
        extra = key_extra(block, bases[s], length)
        scores = dot_nt(query, jnp.concatenate([k_refs[s][0], extra], 1))
        weights = jnp.exp2(scores * COEF).astype(b16)
        total = total + dot_nn(weights, jnp.concatenate([v_refs[s][0], ones], 1))
    sums = total[:, LANES:]
    out_ref[0] = join_heads(total[:, :LANES] / sums)
    whole = (level + jnp.log2(sums)) / COEF
    lane = lane_iota(rows)
    mine = place3(whole[:rows], lane, 6 * pair) + place3(whole[rows:], lane, 6 * pair + 3)

    @pl.when(pair == 0)
    def _():
        extra_ref[0] = jnp.where(lane == MASK_LANE, 1.0, 0.0)

    extra_ref[0] += mine


def corr_kernel(grad_ref, value_ref, extra_ref, out_ref):
    width = grad_ref.shape[1]
    grad = grad_ref[...]
    feature = lax.broadcasted_iota(jnp.int32, (width, LANES), 0) // HEAD_DIM
    lane = lax.broadcasted_iota(jnp.int32, (width, LANES), 1)
    pick = jnp.where(
        (lane >= CORR_LANE) & (feature == (lane - CORR_LANE) // 3), 1.0, 0.0
    ).astype(b16)
    corr = sum(dot_nn(p, pick) for p in split3(grad * value_ref[...]))
    rows = grad.shape[0]
    lane = lane_iota(rows)
    hi, mid, low = (p.astype(f32) for p in split3(corr))
    part = lax.rem(lane, 3)
    placed = jnp.where(part == 0, hi, jnp.where(part == 1, mid, low))
    inside = (lane >= CORR_LANE) & (lane < CORR_LANE + 3 * (width // HEAD_DIM))
    out_ref[:, :width] = grad.astype(b16)
    out_ref[:, width:] = (extra_ref[...] + jnp.where(inside, placed, 0.0)).astype(b16)


def keep_lanes(x, lane, at):
    return jnp.where((lane >= at) & (lane < at + 3), x, jnp.zeros_like(x))


def query_kernel(slots, bases, lengths, q_ref, grad_ref, extra_ref, *refs):
    k_refs, v_refs = refs[:slots], refs[slots : 2 * slots]
    out_ref = refs[2 * slots]
    seq, pair = pl.program_id(0), pl.program_id(1)
    length = lengths[seq]
    block = k_refs[0].shape[1]
    rows = q_ref.shape[1]
    lane = lane_iota(rows)
    extra = extra_ref[0]
    onehot = jnp.where(lane == MASK_LANE, 1.0, 0.0).astype(b16)
    levels = [keep_lanes(extra, lane, 6 * pair + 3 * h) + onehot for h in range(2)]
    corrs = [keep_lanes(extra, lane, CORR_LANE + 6 * pair + 3 * h) for h in range(2)]
    query = jnp.concatenate([stack_heads(q_ref[0]), jnp.concatenate(levels, 0)], 1)
    grad = jnp.concatenate([stack_heads(grad_ref[0]), jnp.concatenate(corrs, 0)], 1)
    total = jnp.zeros((2 * rows, LANES), f32)
    for s in range(slots):
        meet = key_extra(block, bases[s], length)
        keys = k_refs[s][0]
        weights = jnp.exp2(dot_nt(query, jnp.concatenate([keys, meet], 1)) * COEF)
        terms = dot_nt(grad, jnp.concatenate([v_refs[s][0], meet], 1))
        total = total + dot_nn((weights * terms).astype(b16), keys)
    out_ref[0] = (join_heads(total) * SCALE).astype(b16)


def key_kernel(slots, place, lengths, k_ref, v_ref, *refs):
    q_refs, g_refs, e_refs = refs[:slots], refs[slots : 2 * slots], refs[2 * slots : 3 * slots]
    dk_ref, dv_ref = refs[3 * slots :]
    seq, pair = pl.program_id(0), pl.program_id(1)
    length = lengths[seq]
    rows = k_ref.shape[1]
    lane = lane_iota(rows)
    dead = place[0] * rows + lax.broadcasted_iota(jnp.int32, (rows, LANES), 0) >= length
    mask = jnp.where((lane == MASK_LANE) & dead, MASKED, 0.0)
    minus = jnp.full((rows, LANES), -1.0, f32)
    levels = [(keep_lanes(minus, lane, 6 * pair + 3 * h) + mask).astype(b16) for h in range(2)]
    corrs = [keep_lanes(minus, lane, CORR_LANE + 6 * pair + 3 * h).astype(b16) for h in range(2)]
    keys = jnp.concatenate([stack_heads(k_ref[0]), jnp.concatenate(levels, 0)], 1)
    values = jnp.concatenate([stack_heads(v_ref[0]), jnp.concatenate(corrs, 0)], 1)
    dkeys = jnp.zeros((2 * rows, LANES), f32)
    dvalues = jnp.zeros((2 * rows, LANES), f32)
    for s in range(slots):
        query, grad, extra = q_refs[s][0], g_refs[s][0], e_refs[s][0]
        weights = jnp.exp2(dot_nt(keys, jnp.concatenate([query, extra], 1)) * COEF)
        terms = dot_nt(values, jnp.concatenate([grad, extra], 1))
        dvalues = dvalues + dot_nn(weights.astype(b16), grad)
        dkeys = dkeys + dot_nn((weights * terms).astype(b16), query)
    dk_ref[0] = (join_heads(dkeys) * SCALE).astype(b16)
    dv_ref[0] = join_heads(dvalues).astype(b16)


def column(offset):
    return lambda seq, pair, *_: (seq, 0, offset + pair)


def attend_forward(slots_qkv, bases, lengths, safe):
    slots = len(slots_qkv)
    seqs, block, triple = slots_qkv[0].shape
    width = triple // 3
    pairs = width // LANES
    spec = lambda offset: pl.BlockSpec((1, block, LANES), column(offset))
    return pl.pallas_call(
        functools.partial(forward_kernel, slots),
        grid_spec=pltpu.PrefetchScalarGridSpec(
            num_scalar_prefetch=3,
            grid=(seqs, pairs),
            in_specs=[spec(0)] + [spec(pairs)] * slots + [spec(2 * pairs)] * slots,
            out_specs=[spec(0), pl.BlockSpec((1, block, LANES), lambda seq, pair, *_: (seq, 0, 0))],
            scratch_shapes=[pltpu.VMEM((2 * block, LANES), f32)],
        ),
        out_shape=[
            jax.ShapeDtypeStruct((seqs, block, width), f32),
            jax.ShapeDtypeStruct((seqs, block, LANES), f32),
        ],
        compiler_params=pltpu.CompilerParams(vmem_limit_bytes=VMEM),
        cost_estimate=pl.CostEstimate(
            flops=4 * seqs * block * block * slots * width * 4,
            bytes_accessed=slots * seqs * block * width * 4,
            transcendentals=0,
        ),
    )(bases, lengths, safe, slots_qkv[0], *slots_qkv, *slots_qkv)


def attend_query(slots_qkv, grads, bases, lengths):
    slots = len(slots_qkv)
    seqs, block, triple = slots_qkv[0].shape
    width = triple // 3
    pairs = width // LANES
    spec = lambda offset: pl.BlockSpec((1, block, LANES), column(offset))
    last = pl.BlockSpec((1, block, LANES), lambda seq, pair, *_: (seq, 0, pairs))
    return pl.pallas_call(
        functools.partial(query_kernel, slots),
        grid_spec=pltpu.PrefetchScalarGridSpec(
            num_scalar_prefetch=2,
            grid=(seqs, pairs),
            in_specs=[spec(0), spec(0), last] + [spec(pairs)] * slots + [spec(2 * pairs)] * slots,
            out_specs=spec(0),
        ),
        out_shape=jax.ShapeDtypeStruct((seqs, block, width), b16),
        compiler_params=pltpu.CompilerParams(vmem_limit_bytes=VMEM),
        cost_estimate=pl.CostEstimate(
            flops=6 * seqs * block * block * slots * width * 4,
            bytes_accessed=slots * seqs * block * width * 4,
            transcendentals=0,
        ),
    )(bases, lengths, slots_qkv[0], grads, grads, *slots_qkv, *slots_qkv)


def attend_keys(slots_qkv, slots_grads, place, lengths):
    slots = len(slots_qkv)
    seqs, block, triple = slots_qkv[0].shape
    width = triple // 3
    pairs = width // LANES
    spec = lambda offset: pl.BlockSpec((1, block, LANES), column(offset))
    last = pl.BlockSpec((1, block, LANES), lambda seq, pair, *_: (seq, 0, pairs))
    shape = jax.ShapeDtypeStruct((seqs, block, width), b16)
    return pl.pallas_call(
        functools.partial(key_kernel, slots),
        grid_spec=pltpu.PrefetchScalarGridSpec(
            num_scalar_prefetch=2,
            grid=(seqs, pairs),
            in_specs=[spec(pairs), spec(2 * pairs)] + [spec(0)] * (2 * slots) + [last] * slots,
            out_specs=[spec(0), spec(0)],
        ),
        out_shape=[shape, shape],
        compiler_params=pltpu.CompilerParams(vmem_limit_bytes=VMEM),
        cost_estimate=pl.CostEstimate(
            flops=8 * seqs * block * block * slots * width * 4,
            bytes_accessed=slots * seqs * block * width * 4,
            transcendentals=0,
        ),
    )(place, lengths, slots_qkv[0], slots_qkv[0], *slots_qkv, *slots_grads, *slots_grads)


def place_corr(dattended, attended, extra):
    rows, width = dattended.shape
    return pl.pallas_call(
        corr_kernel,
        out_shape=jax.ShapeDtypeStruct((rows, width + LANES), b16),
        compiler_params=pltpu.CompilerParams(vmem_limit_bytes=VMEM),
    )(dattended, attended, extra)


def layer_norm(value, gain, shift):
    mean = jnp.mean(value, axis=-1, keepdims=True)
    centred = value - mean
    spread = jnp.mean(centred * centred, axis=-1, keepdims=True)
    return centred * lax.rsqrt(spread + EPS) * gain + shift


def gelu_exact(value):
    return jax.nn.gelu(value, approximate=False)


def largest_norm(rows3):
    seqs, block, width = rows3.shape
    heads = width // HEAD_DIM
    pick = (jnp.arange(width)[:, None] // HEAD_DIM == jnp.arange(heads)[None]).astype(b16)
    squares = rows3.astype(f32)
    squares = (squares * squares).astype(b16)
    sums = jnp.einsum("sbw,wh->sbh", squares, pick, preferred_element_type=f32)
    return jnp.max(sums, axis=1)


def per_device(
    tokens,
    lengths,
    attend_weight,
    query_bias,
    value_bias,
    mixing_weight,
    mixing_bias,
    first_gain,
    first_shift,
    up_weight,
    up_bias,
    down_weight,
    down_bias,
    second_gain,
    second_shift,
    cotangent,
):
    seqs, block, width = tokens.shape
    rows = seqs * block
    owners = lax.axis_size("fsdp")
    owner = lax.axis_index("fsdp")
    place = lax.axis_index("ctx")

    small = [
        query_bias, value_bias, mixing_bias, first_gain, first_shift,
        down_bias, second_gain, second_shift, up_bias,
    ]
    small_full = lax.all_gather(jnp.concatenate(small), "fsdp", axis=0)
    cuts, at = [], 0
    for part in small:
        size = part.shape[0]
        cuts.append(small_full[:, at : at + size].reshape(-1).astype(f32))
        at += size
    qbias, vbias, mixbias, fgain, fshift, downbias, sgain, sshift, upbias = cuts

    flat = tokens.reshape(rows, width)
    flat_low = flat.astype(b16)
    attend_full = gather_rows(attend_weight, "fsdp")
    token_slots = ring_gather(flat_low.reshape(seqs, block, width), "ctx")
    mixing_full = gather_rows(mixing_weight, "fsdp")
    up_full = gather_rows(up_weight, "fsdp")
    down_full = gather_rows(down_weight, "fsdp")

    bias = jnp.concatenate([qbias, jnp.zeros_like(qbias), vbias])
    slots_qkv = [
        (jnp.dot(t.reshape(rows, width), attend_full, preferred_element_type=f32) + bias)
        .astype(b16)
        .reshape(seqs, block, 3 * width)
        for t in token_slots
    ]
    spots = ring_slots("ctx")
    bases = spots * block
    key_norm = functools.reduce(
        jnp.maximum, [largest_norm(s[..., width : 2 * width]) for s in slots_qkv]
    )
    query_norm = largest_norm(slots_qkv[0][..., :width])
    bound = jnp.sqrt(key_norm * query_norm) * COEF
    safe = jnp.all(bound.reshape(seqs, -1, 2) < SAFE, axis=-1).astype(jnp.int32).reshape(-1)

    attended3, extra = attend_forward(slots_qkv, bases, lengths, safe)
    attended = attended3.reshape(rows, width)
    attended_low = attended.astype(b16)
    mixed = jnp.dot(attended_low, mixing_full, preferred_element_type=f32) + mixbias
    hidden = flat + mixed
    first = layer_norm(hidden, fgain, fshift)
    first_low = first.astype(b16)
    pre = jnp.dot(first_low, up_full, preferred_element_type=f32) + upbias
    act, gelu_back = jax.vjp(gelu_exact, pre)
    act_low = act.astype(b16)
    branch = jnp.dot(act_low, down_full, preferred_element_type=f32) + downbias
    summed = first + branch
    result, second_back = jax.vjp(layer_norm, summed, sgain, sshift)
    dsummed, grad_sgain, grad_sshift = second_back(cotangent.reshape(rows, width))
    dbranch = dsummed.astype(b16)
    dact = jnp.einsum("rd,fd->rf", dbranch, down_full, preferred_element_type=f32)
    dpre = gelu_back(dact)[0].astype(b16)
    dfirst = dsummed + jnp.einsum("rf,df->rd", dpre, up_full, preferred_element_type=f32)
    _, first_back = jax.vjp(layer_norm, hidden, fgain, fshift)
    dhidden, grad_fgain, grad_fshift = first_back(dfirst)
    dmixed = dhidden.astype(b16)
    dattended = jnp.einsum("re,de->rd", dmixed, mixing_full, preferred_element_type=f32)

    grads = place_corr(dattended, attended, extra.reshape(rows, LANES))
    grads = grads.reshape(seqs, block, width + LANES)
    slots_grads = ring_gather(grads, "ctx")

    grad_down = jnp.einsum("rf,rd->fd", act_low, dbranch, preferred_element_type=f32)
    grad_up = jnp.einsum("rd,rf->df", first_low, dpre, preferred_element_type=f32)
    grad_mixing = jnp.einsum("rd,re->de", attended_low, dmixed, preferred_element_type=f32)
    own_down = reduce_rows(grad_down.astype(b16))
    own_up = reduce_rows(grad_up.astype(b16))
    own_mixing = reduce_rows(grad_mixing.astype(b16))

    dquery = attend_query(slots_qkv, grads, bases, lengths)
    dkeys, dvalues = attend_keys(slots_qkv, slots_grads, place.reshape(1), lengths)
    dprojected = jnp.concatenate([dquery, dkeys, dvalues], axis=2).reshape(rows, 3 * width)
    grad_attend = jnp.einsum("rd,re->de", flat_low, dprojected, preferred_element_type=f32)
    own_attend = reduce_rows(grad_attend.astype(b16))
    tokens_grad = dhidden + jnp.einsum(
        "re,de->rd", dprojected, attend_full, preferred_element_type=f32
    )

    def summed_rows(x):
        return jnp.sum(x.astype(f32), axis=0)

    sums = [
        summed_rows(dmixed), grad_fgain, grad_fshift, summed_rows(dbranch),
        grad_sgain, grad_sshift, summed_rows(dpre),
    ]
    early = lax.psum(jnp.concatenate([v.reshape(owners, -1) for v in sums], 1), ("fsdp", "ctx"))
    late = [summed_rows(dquery.reshape(rows, width)), summed_rows(dvalues.reshape(rows, width))]
    late = lax.psum(jnp.concatenate([v.reshape(owners, -1) for v in late], 1), ("fsdp", "ctx"))
    mine = jnp.concatenate(
        [
            lax.dynamic_index_in_dim(late, owner, 0, keepdims=False),
            lax.dynamic_index_in_dim(early, owner, 0, keepdims=False),
        ]
    )
    share = width // owners
    (
        own_qbias, own_vbias, own_mixbias, own_fgain, own_fshift,
        own_downbias, own_sgain, own_sshift,
    ) = (mine[k * share : (k + 1) * share] for k in range(8))
    own_upbias = mine[8 * share :]
    return (
        result.reshape(seqs, block, width),
        tokens_grad.reshape(seqs, block, width),
        own_attend,
        own_qbias,
        own_vbias,
        own_mixing,
        own_mixbias,
        own_fgain,
        own_fshift,
        own_up,
        own_upbias,
        own_down,
        own_downbias,
        own_sgain,
        own_sshift,
    )


def solution(mesh):
    rows = P("fsdp", "ctx", None)
    matrix = P("fsdp", None)
    vector = P("fsdp")
    return jax.shard_map(
        per_device,
        mesh=mesh,
        in_specs=(
            rows, vector, matrix, vector, vector, matrix, vector, vector, vector,
            matrix, vector, matrix, vector, vector, vector, rows,
        ),
        out_specs=(
            rows, rows, matrix, vector, vector, matrix, vector, vector, vector,
            matrix, vector, matrix, vector, vector, vector,
        ),
        check_vma=False,
    )
```

```python
import functools
import math

import jax
import jax.numpy as jnp
from jax import lax
from jax.experimental import pallas as pl
from jax.experimental.pallas import tpu as pltpu
from jax.sharding import PartitionSpec as P

HEAD_DIM = 64
LANES = 128
EPS = 1e-12
SCALE = 0.125
LOG2E = math.log2(math.e)
COEF = SCALE * LOG2E
MASKED = -1e30
SAFE = 60.0
LOWEST = -1e9
MASK_LANE = 127
CORR_LANE = 36
VMEM = 48 * 1024 * 1024

f32 = jnp.float32
b16 = jnp.bfloat16


def together(*values):
    return lax.optimization_barrier(values)


def swap(x, axis, bit):
    count = lax.axis_size(axis)
    return lax.ppermute(x, axis, [(i, i ^ bit) for i in range(count)])


def bits_of(count):
    return [1 << k for k in range(count.bit_length() - 1)]


def ring_order(count):
    half = count // 2
    return [2 * p if p < half else 2 * (count - 1 - p) + 1 for p in range(count)]


def ring_slots(axis):
    count = lax.axis_size(axis)
    order = jnp.asarray(ring_order(count), jnp.int32)
    place = lax.axis_index(axis)
    spot = jnp.where(place % 2 == 0, place // 2, count - 1 - place // 2)
    steps = [0]
    for s in range(1, count // 2):
        steps += [-s, s]
    steps.append(count // 2)
    return order[jnp.mod(spot + jnp.asarray(steps, jnp.int32), count)]


def ring_step(r, l, axis):
    count = lax.axis_size(axis)
    order = ring_order(count)
    right = [(order[p], order[(p + 1) % count]) for p in range(count)]
    left = [(d, s) for s, d in right]
    return lax.ppermute(r, axis, right), lax.ppermute(l, axis, left)


def ring_last(r, l, axis):
    return ring_step(r[:1], l[1:], axis)


def across(w, axis):
    blocks = {0: w}
    for bit in bits_of(lax.axis_size(axis))[1:]:
        blocks |= {k ^ bit: swap(v, axis, bit) for k, v in list(blocks.items())}
    return blocks


def between(blocks, axis):
    keys = list(blocks)
    got = swap(jnp.stack([blocks[k] for k in keys]), axis, 1)
    return blocks | {k ^ 1: got[i] for i, k in enumerate(keys)}


def in_order(blocks, axis):
    i = lax.axis_index(axis)
    count = lax.axis_size(axis)
    now = [blocks[k] for k in range(count)]
    for bit in bits_of(count):
        low = (i // bit) % 2 == 0
        now = [jnp.where(low, now[k], now[k ^ bit]) for k in range(count)]
    return jnp.concatenate(now, 0)


def added(keep, got):
    return (keep.astype(f32) + got.astype(f32)).astype(b16)


def core_parts(g):
    core = lax.axis_index("fsdp") % 2
    pairs = g.reshape((-1, 2) + g.shape[1:])
    send = lax.dynamic_index_in_dim(pairs, 1 - core, 1, keepdims=False)
    keep = lax.dynamic_index_in_dim(pairs, core, 1, keepdims=False)
    return send, keep


def chip_sum(x):
    bits = bits_of(lax.axis_size("fsdp"))[1:]
    for bit in bits[::-1]:
        upper = (lax.axis_index("fsdp") // bit) % 2
        pairs = x.reshape((2, -1) + x.shape[1:])
        send = lax.dynamic_index_in_dim(pairs, 1 - upper, 0, keepdims=False)
        keep = lax.dynamic_index_in_dim(pairs, upper, 0, keepdims=False)
        x = added(keep, swap(send, "fsdp", bit))
    return x[0]


def halve(x, axis, bit):
    upper = (lax.axis_index(axis) // bit) % 2
    half = x.shape[0] // 2
    send = lax.dynamic_slice_in_dim(x, (1 - upper) * half, half, 0)
    keep = lax.dynamic_slice_in_dim(x, upper * half, half, 0)
    return added(keep, swap(send, axis, bit))


def unhalve(x, axis, bit):
    low = (lax.axis_index(axis) // bit) % 2 == 0
    other = swap(x, axis, bit)
    return jnp.concatenate([jnp.where(low, x, other), jnp.where(low, other, x)], 0)


def block_sum_steps(blocks):
    first = bits_of(blocks)
    second = [first[1], first[0]] + first[2:]

    def down(k):
        return lambda ab: (halve(ab[0], "ctx", first[k]), halve(ab[1], "ctx", second[k]))

    def up(k):
        return lambda ab: (unhalve(ab[0], "ctx", first[k]), unhalve(ab[1], "ctx", second[k]))

    count = len(first)
    return [down(k) for k in range(count)] + [up(k) for k in range(count)][::-1]


def columns_to_rows(x, width):
    return jnp.concatenate(
        [x[..., k * width : (k + 1) * width] for k in range(x.shape[-1] // width)], axis=-2
    )


def rows_to_columns(x, count):
    rows = x.shape[0] // count
    return jnp.concatenate([x[k * rows : (k + 1) * rows] for k in range(count)], axis=1)


def row_pad(rows, blocks):
    unit = 8 * blocks
    return -rows % unit


def dot_nt(a, b):
    return lax.dot_general(a, b, (((1,), (1,)), ((), ())), preferred_element_type=f32)


def dot_nn(a, b):
    return lax.dot_general(a, b, (((1,), (0,)), ((), ())), preferred_element_type=f32)


def lane_iota(rows):
    return lax.broadcasted_iota(jnp.int32, (rows, LANES), 1)


def split3(x):
    hi = x.astype(b16)
    rest = x - hi.astype(f32)
    mid = rest.astype(b16)
    low = (rest - mid.astype(f32)).astype(b16)
    return hi, mid, low


def place3(x, lane, at):
    hi, mid, low = (p.astype(f32) for p in split3(x))
    zero = jnp.zeros_like(x)
    return jnp.where(
        lane == at, hi, jnp.where(lane == at + 1, mid, jnp.where(lane == at + 2, low, zero))
    )


def stack_heads(pair):
    rows = pair.shape[0]
    lane = lane_iota(rows)
    zero = jnp.zeros_like(pair)
    return jnp.concatenate(
        [jnp.where(lane < HEAD_DIM, pair, zero), jnp.where(lane >= HEAD_DIM, pair, zero)], 0
    )


def join_heads(x):
    rows = x.shape[0] // 2
    return jnp.where(lane_iota(rows) < HEAD_DIM, x[:rows], x[rows:])


def key_extra(rows, base, length):
    lane = lane_iota(rows)
    dead = base + lax.broadcasted_iota(jnp.int32, (rows, LANES), 0) >= length
    mask = jnp.where(dead, MASKED, 0.0)
    return jnp.where(lane == MASK_LANE, mask, -1.0).astype(b16)


def spread_heads(x):
    rows = x.shape[0]
    lane = lane_iota(rows)
    other = pltpu.roll(x, HEAD_DIM, 1)
    return jnp.concatenate(
        [jnp.where(lane < HEAD_DIM, x, other), jnp.where(lane < HEAD_DIM, other, x)], 0
    )


def pair_columns(pair):
    return pl.ds(pl.multiple_of(pair * LANES, LANES), LANES)


def forward_kernel(slots, begin, final, bases, lengths, safe, q_ref, *refs):
    k_refs, v_refs = refs[:slots], refs[slots : 2 * slots]
    refs = refs[2 * slots :]
    if not begin:
        numer_in, sums_in, level_in = refs[:3]
        refs = refs[3:]
    if final:
        out_ref, extra_ref, level_ref, lanes_ref, meet_ref = refs
    else:
        numer_out, sums_out, level_out, level_ref, lanes_ref, meet_ref = refs
    seq = pl.program_id(0)
    length = lengths[seq]
    rows = q_ref.shape[1]
    block = k_refs[0].shape[1]
    pairs = q_ref.shape[2] // LANES
    lane2 = lane_iota(2 * rows)
    lane = lane_iota(rows)
    onehot = jnp.where(lane2 == MASK_LANE, 1.0, 0.0)
    for s in range(slots):
        meet_ref[s] = key_extra(block, bases[s], length)
    if final:
        extra_ref[0] = jnp.where(lane == MASK_LANE, 1.0, 0.0)

    def one_pair(pair, carry):
        cols = pair_columns(pair)
        stacked = stack_heads(q_ref[0, :, cols])
        level_ref[...] = jnp.zeros_like(level_ref)
        lanes_ref[...] = onehot.astype(b16)

        @pl.when(safe[seq * pairs + pair] == 0)
        def _():
            top = jnp.full((2 * rows, 1), MASKED, f32)
            probe = jnp.concatenate([stacked, onehot.astype(b16)], 1)
            for s in range(slots):
                scores = dot_nt(probe, jnp.concatenate([k_refs[s][0, :, cols], meet_ref[s]], 1))
                top = jnp.maximum(top, jnp.max(scores, axis=1, keepdims=True))
            before = LOWEST if begin else spread_heads(level_in[0, :, cols])
            level = jnp.maximum(before, jnp.ceil(top * COEF))
            lanes_ref[...] = (place3(level / COEF, lane2, 0) + onehot).astype(b16)
            level_ref[...] = join_heads(jnp.broadcast_to(level, (2 * rows, LANES)))

        query = jnp.concatenate([stacked, lanes_ref[...]], 1)
        ones = jnp.ones((block, LANES), b16)
        total = jnp.zeros((2 * rows, 2 * LANES), f32)
        for s in range(slots):
            scores = dot_nt(query, jnp.concatenate([k_refs[s][0, :, cols], meet_ref[s]], 1))
            weights = jnp.exp2(scores * COEF).astype(b16)
            total = total + dot_nn(weights, jnp.concatenate([v_refs[s][0, :, cols], ones], 1))
        numer, sums, now = join_heads(total[:, :LANES]), join_heads(total[:, LANES:]), level_ref[...]
        if not begin:
            factor = jnp.exp2(level_in[0, :, cols] - now)
            numer = numer + numer_in[0, :, cols] * factor
            sums = sums + sums_in[0, :, cols] * factor
        if not final:
            numer_out[0, :, cols] = numer
            sums_out[0, :, cols] = sums
            level_out[0, :, cols] = now
            return carry
        out_ref[0, :, cols] = numer / sums
        whole = spread_heads((now + jnp.log2(sums)) / COEF)
        extra_ref[0] += place3(whole[:rows], lane, 6 * pair) + place3(
            whole[rows:], lane, 6 * pair + 3
        )
        return carry

    lax.fori_loop(0, pairs, one_pair, 0)


def corr_kernel(grad_ref, value_ref, extra_ref, out_ref):
    width = grad_ref.shape[1]
    grad = grad_ref[...]
    feature = lax.broadcasted_iota(jnp.int32, (width, LANES), 0) // HEAD_DIM
    lane = lax.broadcasted_iota(jnp.int32, (width, LANES), 1)
    pick = jnp.where(
        (lane >= CORR_LANE) & (feature == (lane - CORR_LANE) // 3), 1.0, 0.0
    ).astype(b16)
    corr = sum(dot_nn(p, pick) for p in split3(grad * value_ref[...]))
    rows = grad.shape[0]
    lane = lane_iota(rows)
    hi, mid, low = (p.astype(f32) for p in split3(corr))
    part = lax.rem(lane, 3)
    placed = jnp.where(part == 0, hi, jnp.where(part == 1, mid, low))
    inside = (lane >= CORR_LANE) & (lane < CORR_LANE + 3 * (width // HEAD_DIM))
    out_ref[:, :width] = grad.astype(b16)
    out_ref[:, width:] = (extra_ref[...] + jnp.where(inside, placed, 0.0)).astype(b16)


def keep_lanes(x, lane, at):
    return jnp.where((lane >= at) & (lane < at + 3), x, jnp.zeros_like(x))


def query_kernel(slots, bases, lengths, q_ref, grad_ref, extra_ref, *refs):
    k_refs, v_refs = refs[:slots], refs[slots : 2 * slots]
    out_ref, meet_ref = refs[2 * slots :]
    seq = pl.program_id(0)
    length = lengths[seq]
    block = k_refs[0].shape[1]
    rows = q_ref.shape[1]
    lane = lane_iota(rows)
    onehot = jnp.where(lane == MASK_LANE, 1.0, 0.0).astype(b16)
    for s in range(slots):
        meet_ref[s] = key_extra(block, bases[s], length)

    def one_pair(pair, carry):
        cols = pair_columns(pair)
        extra = extra_ref[0]
        levels = [keep_lanes(extra, lane, 6 * pair + 3 * h) + onehot for h in range(2)]
        corrs = [keep_lanes(extra, lane, CORR_LANE + 6 * pair + 3 * h) for h in range(2)]
        query = jnp.concatenate([stack_heads(q_ref[0, :, cols]), jnp.concatenate(levels, 0)], 1)
        grad = jnp.concatenate([stack_heads(grad_ref[0, :, cols]), jnp.concatenate(corrs, 0)], 1)
        total = jnp.zeros((2 * rows, LANES), f32)
        for s in range(slots):
            meet = meet_ref[s]
            keys = k_refs[s][0, :, cols]
            weights = jnp.exp2(dot_nt(query, jnp.concatenate([keys, meet], 1)) * COEF)
            terms = dot_nt(grad, jnp.concatenate([v_refs[s][0, :, cols], meet], 1))
            total = total + dot_nn((weights * terms).astype(b16), keys)
        out_ref[0, :, cols] = (join_heads(total) * SCALE).astype(b16)
        return carry

    lax.fori_loop(0, q_ref.shape[2] // LANES, one_pair, 0)


def key_kernel(slots, begin, final, place, lengths, k_ref, v_ref, *refs):
    q_refs, g_refs, e_refs = refs[:slots], refs[slots : 2 * slots], refs[2 * slots : 3 * slots]
    refs = refs[3 * slots :]
    if not begin:
        dk_in, dv_in = refs[:2]
        refs = refs[2:]
    dk_ref, dv_ref = refs
    length = lengths[pl.program_id(0)]
    rows = k_ref.shape[1]
    lane = lane_iota(rows)
    dead = place[0] * rows + lax.broadcasted_iota(jnp.int32, (rows, LANES), 0) >= length
    mask = jnp.where((lane == MASK_LANE) & dead, MASKED, 0.0)
    minus = jnp.full((rows, LANES), -1.0, f32)

    def one_pair(pair, carry):
        cols = pair_columns(pair)
        levels = [(keep_lanes(minus, lane, 6 * pair + 3 * h) + mask).astype(b16) for h in range(2)]
        corrs = [
            keep_lanes(minus, lane, CORR_LANE + 6 * pair + 3 * h).astype(b16) for h in range(2)
        ]
        keys = jnp.concatenate([stack_heads(k_ref[0, :, cols]), jnp.concatenate(levels, 0)], 1)
        values = jnp.concatenate([stack_heads(v_ref[0, :, cols]), jnp.concatenate(corrs, 0)], 1)
        dkeys = jnp.zeros((2 * rows, LANES), f32)
        dvalues = jnp.zeros((2 * rows, LANES), f32)
        for s in range(slots):
            query, grad, extra = q_refs[s][0, :, cols], g_refs[s][0, :, cols], e_refs[s][0]
            weights = jnp.exp2(dot_nt(keys, jnp.concatenate([query, extra], 1)) * COEF)
            terms = dot_nt(values, jnp.concatenate([grad, extra], 1))
            dvalues = dvalues + dot_nn(weights.astype(b16), grad)
            dkeys = dkeys + dot_nn((weights * terms).astype(b16), query)
        dk, dv = join_heads(dkeys) * SCALE, join_heads(dvalues)
        if not begin:
            dk, dv = dk + dk_in[0, :, cols], dv + dv_in[0, :, cols]
        dk_ref[0, :, cols] = dk.astype(dk_ref.dtype)
        dv_ref[0, :, cols] = dv.astype(dv_ref.dtype)
        return carry

    lax.fori_loop(0, k_ref.shape[2] // LANES, one_pair, 0)


def third(block, width, which, seq_at=0):
    return pl.BlockSpec((1, block, width), lambda seq, *_: (seq_at + seq, 0, which))


def lanes_spec(block, at, seq_at=0):
    return pl.BlockSpec((1, block, LANES), lambda seq, *_: (seq_at + seq, 0, at))


def cost(matmuls, seqs, block, slots, width):
    return pl.CostEstimate(
        flops=8 * matmuls * seqs * block * block * slots * width,
        bytes_accessed=slots * seqs * block * width * 4,
        transcendentals=0,
    )


def attend_forward(own, slots_qkv, bases, lengths, safe, state=(), final=False):
    slots = len(slots_qkv)
    seqs, block, triple = own.shape
    width = triple // 3
    q, k, v = (third(block, width, n) for n in range(3))
    part = jax.ShapeDtypeStruct((seqs, block, width), f32)
    if final:
        shapes = [part, jax.ShapeDtypeStruct((seqs, block, LANES), f32)]
        outs = [q, lanes_spec(block, 0)]
    else:
        shapes, outs = [part] * 3, [q] * 3
    return pl.pallas_call(
        functools.partial(forward_kernel, slots, not state, final),
        grid_spec=pltpu.PrefetchScalarGridSpec(
            num_scalar_prefetch=3,
            grid=(seqs,),
            in_specs=[q] + [k] * slots + [v] * slots + [q] * len(state),
            out_specs=outs,
            scratch_shapes=[
                pltpu.VMEM((block, LANES), f32),
                pltpu.VMEM((2 * block, LANES), b16),
                pltpu.VMEM((slots, block, LANES), b16),
            ],
        ),
        out_shape=shapes,
        compiler_params=pltpu.CompilerParams(vmem_limit_bytes=VMEM),
        cost_estimate=cost(2, seqs, block, slots, width),
    )(bases, lengths, safe, own, *slots_qkv, *slots_qkv, *state)


def attend_query(seq_at, count, slots_qkv, grads, bases, lengths):
    slots = len(slots_qkv)
    block, triple = slots_qkv[0].shape[1:]
    width = triple // 3
    q, k, v = (third(block, width, n, seq_at) for n in range(3))
    return pl.pallas_call(
        functools.partial(query_kernel, slots),
        grid_spec=pltpu.PrefetchScalarGridSpec(
            num_scalar_prefetch=2,
            grid=(count,),
            in_specs=[q, q, lanes_spec(block, width // LANES, seq_at)]
            + [k] * slots
            + [v] * slots,
            out_specs=third(block, width, 0),
            scratch_shapes=[pltpu.VMEM((slots, block, LANES), b16)],
        ),
        out_shape=jax.ShapeDtypeStruct((count, block, width), b16),
        compiler_params=pltpu.CompilerParams(vmem_limit_bytes=VMEM),
        cost_estimate=cost(3, count, block, slots, width),
    )(bases, lengths[seq_at : seq_at + count], slots_qkv[0], grads, grads, *slots_qkv, *slots_qkv)


def attend_keys(own, slots_qkv, slots_grads, place, lengths, state=(), final=False):
    slots = len(slots_qkv)
    seqs, block, triple = own.shape
    width = triple // 3
    q, k, v = (third(block, width, n) for n in range(3))
    shape = jax.ShapeDtypeStruct((seqs, block, width), b16 if final else f32)
    return pl.pallas_call(
        functools.partial(key_kernel, slots, not state, final),
        grid_spec=pltpu.PrefetchScalarGridSpec(
            num_scalar_prefetch=2,
            grid=(seqs,),
            in_specs=[k, v]
            + [q] * (2 * slots)
            + [lanes_spec(block, width // LANES)] * slots
            + [q] * len(state),
            out_specs=[q, q],
        ),
        out_shape=[shape, shape],
        compiler_params=pltpu.CompilerParams(vmem_limit_bytes=VMEM),
        cost_estimate=cost(4, seqs, block, slots, width),
    )(place, lengths, own, own, *slots_qkv, *slots_grads, *slots_grads, *state)


def place_corr(dattended, attended, extra):
    rows, width = dattended.shape
    return pl.pallas_call(
        corr_kernel,
        out_shape=jax.ShapeDtypeStruct((rows, width + LANES), b16),
        compiler_params=pltpu.CompilerParams(vmem_limit_bytes=VMEM),
    )(dattended, attended, extra)


def layer_norm(value, gain, shift):
    mean = jnp.mean(value, axis=-1, keepdims=True)
    centred = value - mean
    spread = jnp.mean(centred * centred, axis=-1, keepdims=True)
    return centred * lax.rsqrt(spread + EPS) * gain + shift


def gelu_exact(value):
    return jax.nn.gelu(value, approximate=False)


def largest_norm(rows3):
    seqs, block, width = rows3.shape
    heads = width // HEAD_DIM
    pick = (jnp.arange(width)[:, None] // HEAD_DIM == jnp.arange(heads)[None]).astype(b16)
    squares = rows3.astype(f32)
    squares = (squares * squares).astype(b16)
    sums = jnp.einsum("sbw,wh->sbh", squares, pick, preferred_element_type=f32)
    return jnp.max(sums, axis=1)


def per_device(
    tokens,
    lengths,
    attend_weight,
    query_bias,
    value_bias,
    mixing_weight,
    mixing_bias,
    first_gain,
    first_shift,
    up_weight,
    up_bias,
    down_weight,
    down_bias,
    second_gain,
    second_shift,
    cotangent,
):
    seqs, block, width = tokens.shape
    rows = seqs * block
    owners = lax.axis_size("fsdp")
    blocks = lax.axis_size("ctx")
    place = lax.axis_index("ctx")
    share = width // owners
    steps = blocks // 2

    flat = tokens.reshape(rows, width)
    flat_low = flat.astype(b16)
    own_tokens = flat_low.reshape(seqs, block, width)

    small = jnp.concatenate(
        [query_bias, value_bias, mixing_bias, first_gain, first_shift, down_bias,
         second_gain, second_shift, up_bias]
    )
    small_rows = -(-small.shape[0] // (16 * width)) * 16
    small = jnp.pad(small, (0, small_rows * width - small.shape[0])).reshape(small_rows, width)
    mixing_more = jnp.concatenate([mixing_weight, small], 0)

    spots = ring_slots("ctx")
    bases = spots * block

    def pick(blocks_at):
        keys = list(blocks_at)
        return keys, [blocks_at[k] for k in keys]

    tr, tl = ring_step(own_tokens, own_tokens, "ctx")
    keys, got = pick(across(attend_weight, "fsdp"))
    tr, tl, mixing_more, up_weight, *got = together(tr, tl, mixing_more, up_weight, *got)
    attend_blocks = dict(zip(keys, got))
    token_slots = [own_tokens, tr, tl]

    def project(t):
        out = jnp.dot(t.reshape(rows, width), attend_full, preferred_element_type=f32) + bias
        return out.astype(b16).reshape(seqs, block, 3 * width)

    attend_blocks = between(attend_blocks, "fsdp")
    tr, tl = ring_step(tr, tl, "ctx")
    _, mixing_got = pick(across(mixing_more, "fsdp"))
    _, up_got = pick(across(up_weight, "fsdp"))
    attend_full = in_order(attend_blocks, "fsdp")
    tr, tl, attend_full, *mixing_got = together(tr, tl, attend_full, *mixing_got)
    token_slots += [tr, tl]

    mixing_blocks = between(dict(zip(keys, mixing_got)), "fsdp")
    mixing_all = in_order(mixing_blocks, "fsdp").reshape(owners, share + small_rows, width)
    mixing_full = mixing_all[:, :share].reshape(width, width)
    small_full = mixing_all[:, share:].reshape(owners, -1).astype(f32)
    vectors = small_full[:, : 8 * share].reshape(owners, 8, share).transpose(1, 0, 2)
    vectors = vectors.reshape(8, width)
    qbias, vbias, mixbias, fgain, fshift, downbias, sgain, sshift = (
        vectors[k : k + 1] for k in range(8)
    )
    upbias = small_full[:, 8 * share : 8 * share + up_bias.shape[0]].reshape(1, -1)
    bias = jnp.concatenate([qbias, jnp.zeros_like(qbias), vbias], 1)

    def flags(query_norm, slots):
        norm = functools.reduce(
            jnp.maximum, [largest_norm(v[..., width : 2 * width]) for v in slots]
        )
        bound = jnp.sqrt(norm * query_norm) * COEF
        return jnp.all(bound.reshape(seqs, -1, 2) < SAFE, axis=-1).reshape(-1)

    slots_qkv = []
    for step in range(3, steps + 1):
        last = step == steps
        nr, nl = ring_last(tr, tl, "ctx") if last else ring_step(tr, tl, "ctx")
        slots_qkv += [project(t) for t in token_slots[len(slots_qkv) : 2 * step - 1]]
        if last:
            _, down_got = pick(across(down_weight, "fsdp"))
            up_blocks = between(dict(zip(keys, up_got)), "fsdp")
            query_norm = largest_norm(slots_qkv[0][..., :width])
            safe = flags(query_norm, slots_qkv)
            state = attend_forward(
                slots_qkv[0], slots_qkv, bases[: len(slots_qkv)], lengths, safe.astype(jnp.int32)
            )
            tr, tl, *state = together(nr, nl, *state)
            token_slots.append(jnp.concatenate([tr, tl], 0))
        else:
            tr, tl, down_weight, *rest = together(nr, nl, down_weight, *up_got, *slots_qkv)
            up_got, slots_qkv = rest[: len(up_got)], rest[len(up_got) :]
            token_slots += [tr, tl]
    done = len(slots_qkv)
    slots_qkv += [project(t) for t in token_slots[done:]]
    safe &= flags(query_norm, slots_qkv[done:])
    attended3, extra = attend_forward(
        slots_qkv[0], slots_qkv[done:], bases[done:], lengths, safe.astype(jnp.int32),
        tuple(state), True,
    )
    up_full = in_order(up_blocks, "fsdp")
    down_full = in_order(between(dict(zip(keys, down_got)), "fsdp"), "fsdp")

    attended = attended3.reshape(rows, width)
    attended_low = attended.astype(b16)
    mixed = jnp.dot(attended_low, mixing_full, preferred_element_type=f32) + mixbias
    hidden = flat + mixed
    first = layer_norm(hidden, fgain, fshift)
    first_low = first.astype(b16)
    pre = jnp.dot(first_low, up_full, preferred_element_type=f32) + upbias
    act, gelu_back = jax.vjp(gelu_exact, pre)
    act_low = act.astype(b16)
    branch = jnp.dot(act_low, down_full, preferred_element_type=f32) + downbias
    summed = first + branch
    result, second_back = jax.vjp(layer_norm, summed, sgain, sshift)
    dsummed, grad_sgain, grad_sshift = second_back(cotangent.reshape(rows, width))
    dbranch = dsummed.astype(b16)
    dact = jnp.einsum("rd,fd->rf", dbranch, down_full, preferred_element_type=f32)
    dpre = gelu_back(dact)[0].astype(b16)
    dfirst = dsummed + jnp.einsum("rf,df->rd", dpre, up_full, preferred_element_type=f32)
    _, first_back = jax.vjp(layer_norm, hidden, fgain, fshift)
    dhidden, grad_fgain, grad_fshift = first_back(dfirst)
    dmixed = dhidden.astype(b16)
    dattended = jnp.einsum("re,de->rd", dmixed, mixing_full, preferred_element_type=f32)

    grads = place_corr(dattended, attended, extra.reshape(rows, LANES))
    grads = grads.reshape(seqs, block, width + LANES)
    grads, act_low, dbranch, first_low, dpre, attended_low, dmixed = together(
        grads, act_low, dbranch, first_low, dpre, attended_low, dmixed
    )

    def summed_rows(x):
        return jnp.sum(x.astype(f32), axis=0)

    def vector_rows(vectors):
        flat_vectors = jnp.concatenate([v.reshape(owners, -1) for v in vectors], 1)
        need = -(-flat_vectors.shape[1] // width)
        need += row_pad(need, blocks)
        pad = need * width - flat_vectors.shape[1]
        return jnp.pad(flat_vectors, ((0, 0), (0, pad))).astype(b16).reshape(owners, need, width)

    steps_ctx = block_sum_steps(blocks)

    def begin_sum(x):
        more = row_pad(x.shape[0], blocks)
        x = jnp.pad(x, ((0, more), (0, 0))) if more else x
        return x[:, : width // 2], x[:, width // 2 :]

    place1 = place.reshape(1)

    gr, gl = ring_step(grads, grads, "ctx")
    grad_down = jnp.einsum("rf,rd->fd", act_low, dbranch, preferred_element_type=f32).astype(b16)
    down_send, down_keep = core_parts(grad_down.reshape(owners, -1, width))
    down_got = swap(down_send, "fsdp", 1)
    grad_mixing = jnp.einsum("rd,re->de", attended_low, dmixed, preferred_element_type=f32)
    early = vector_rows(
        [summed_rows(dmixed), grad_fgain, grad_fshift, summed_rows(dbranch), grad_sgain,
         grad_sshift, summed_rows(dpre)]
    )
    grad_mixing = jnp.concatenate(
        [grad_mixing.astype(b16).reshape(owners, share, width), early], 1
    )
    mixing_send, mixing_keep = core_parts(grad_mixing)
    mixing_got = swap(mixing_send, "fsdp", 1)
    grad_up = jnp.einsum("rd,rf->df", first_low, dpre, preferred_element_type=f32).astype(b16)
    dquery = [attend_query(0, 1, slots_qkv, grads, bases, lengths)]
    gr, gl, down_got, mixing_got, grad_up, grads, dquery[0] = together(
        gr, gl, down_got, mixing_got, grad_up, grads, dquery[0]
    )
    grad_slots = [grads, gr, gl]

    gr, gl = ring_step(gr, gl, "ctx")
    sum_one = jnp.concatenate([added(down_keep, down_got), added(mixing_keep, mixing_got)], 1)
    sum_one = chip_sum(sum_one)
    up_send, up_keep = core_parts(grad_up.reshape(owners, share, -1))
    up_got = swap(up_send, "fsdp", 1)
    dquery.append(attend_query(1, 1, slots_qkv, grads, bases, lengths))
    gr, gl, up_got, dquery[1] = together(gr, gl, up_got, dquery[1])
    grad_slots += [gr, gl]
    dquery = jnp.concatenate(dquery, 0).reshape(rows, width)

    dkv = ()
    done = 0
    for step in range(3, steps + 1):
        last = step == steps
        nr, nl = ring_last(gr, gl, "ctx") if last else ring_step(gr, gl, "ctx")
        if step == 3:
            grad_query = jnp.einsum("rd,re->de", flat_low, dquery, preferred_element_type=f32)
            query_send, query_keep = core_parts(grad_query.astype(b16).reshape(owners, share, width))
            query_got = swap(query_send, "fsdp", 1)
        if last:
            sum_two = jnp.concatenate(
                [columns_to_rows(added(up_keep, up_got), width), added(query_keep, query_got)], 1
            )
            sum_two = chip_sum(sum_two)
            one = steps_ctx[0](begin_sum(sum_one))
        use = slice(done, len(grad_slots))
        dkv = attend_keys(
            slots_qkv[0], slots_qkv[use], grad_slots[use], place1, lengths, tuple(dkv)
        )
        done = len(grad_slots)
        if last:
            gr, gl, *rest = together(nr, nl, *one, *dkv)
            one, dkv = tuple(rest[:2]), rest[2:]
            grad_slots.append(jnp.concatenate([gr, gl], 0))
        else:
            gr, gl, sum_one, query_got, *dkv = together(nr, nl, sum_one, query_got, *dkv)
            grad_slots += [gr, gl]

    use = slice(done, len(grad_slots))
    one = steps_ctx[1](one)
    dkeys, dvalues = attend_keys(
        slots_qkv[0], slots_qkv[use], grad_slots[use], place1, lengths, tuple(dkv), True
    )
    dkeys, dvalues, one0, one1, sum_two = together(dkeys, dvalues, *one, sum_two)
    one = (one0, one1)
    dkeys, dvalues = dkeys.reshape(rows, width), dvalues.reshape(rows, width)
    dlate = jnp.concatenate([dkeys, dvalues], 1)
    grad_late = jnp.einsum("rd,re->de", flat_low, dlate, preferred_element_type=f32).astype(b16)
    grad_late = columns_to_rows(grad_late.reshape(owners, share, -1), width)
    late = vector_rows([summed_rows(dquery), summed_rows(dvalues)])
    late_send, late_keep = core_parts(jnp.concatenate([grad_late, late], 1))
    late_got = swap(late_send, "fsdp", 1)
    one = steps_ctx[2](one)
    dprojected = jnp.concatenate([dquery, dlate], 1)
    tokens_grad = dhidden + jnp.einsum(
        "re,de->rd", dprojected, attend_full, preferred_element_type=f32
    )
    late_got, sum_two, *one = together(late_got, sum_two, *one)

    two = begin_sum(sum_two)
    sum_late = chip_sum(added(late_keep, late_got))
    one = steps_ctx[3](one)
    two = steps_ctx[0](two)
    sum_late, *both = together(sum_late, *one, *two)
    chains = [(tuple(both[:2]), 4), (tuple(both[2:]), 1), (begin_sum(sum_late), 0)]
    while any(at < len(steps_ctx) for _, at in chains):
        chains = [
            (steps_ctx[at](pair), at + 1) if at < len(steps_ctx) else (pair, at)
            for pair, at in chains
        ]
        flat_chains = together(*(v for pair, _ in chains for v in pair))
        chains = [
            ((flat_chains[2 * k], flat_chains[2 * k + 1]), at)
            for k, (_, at) in enumerate(chains)
        ]
    one, two, three = (jnp.concatenate(pair, 1).astype(f32) for pair, _ in chains)

    at = down_weight.shape[0]
    own_down = one[:at]
    own_mixing = one[at : at + share]
    early = one[at + share : at + share + early.shape[1]].reshape(-1)
    parts = up_weight.shape[1] // width
    own_up = rows_to_columns(two[: parts * share], parts)
    own_query = two[parts * share : (parts + 1) * share]
    own_attend = jnp.concatenate([own_query, rows_to_columns(three[: 2 * share], 2)], 1)
    late = three[2 * share : 2 * share + late.shape[1]].reshape(-1)
    own_qbias, own_vbias = (late[k * share : (k + 1) * share] for k in range(2))
    own_mixbias, own_fgain, own_fshift, own_downbias, own_sgain, own_sshift = (
        early[k * share : (k + 1) * share] for k in range(6)
    )
    own_upbias = early[6 * share : 6 * share + up_bias.shape[0]]
    return (
        result.reshape(seqs, block, width),
        tokens_grad.reshape(seqs, block, width),
        own_attend,
        own_qbias,
        own_vbias,
        own_mixing,
        own_mixbias,
        own_fgain,
        own_fshift,
        own_up,
        own_upbias,
        own_down,
        own_downbias,
        own_sgain,
        own_sshift,
    )


def solution(mesh):
    rows = P("fsdp", "ctx", None)
    matrix = P("fsdp", None)
    vector = P("fsdp")
    return jax.shard_map(
        per_device,
        mesh=mesh,
        in_specs=(
            rows, vector, matrix, vector, vector, matrix, vector, vector, vector,
            matrix, vector, matrix, vector, vector, vector, rows,
        ),
        out_specs=(
            rows, rows, matrix, vector, vector, matrix, vector, vector, vector,
            matrix, vector, matrix, vector, vector, vector,
        ),
        check_vma=False,
    )
```

```python
import functools
import math

import jax
import jax.numpy as jnp
from jax import lax
from jax.experimental import pallas as pl
from jax.experimental.pallas import tpu as pltpu
from jax.sharding import PartitionSpec as P

HEAD_DIM = 64
LANES = 128
EPS = 1e-12
SCALE = 0.125
LOG2E = math.log2(math.e)
COEF = SCALE * LOG2E
MASKED = -1e30
SAFE = 60.0
LOWEST = -1e9
MASK_LANE = 127
CORR_LANE = 36
VMEM = 30 * 1024 * 1024
VMEM_BACK = 52 * 1024 * 1024

f32 = jnp.float32
b16 = jnp.bfloat16


def together(*values):
    return lax.optimization_barrier(values)


def swap(x, axis, bit):
    count = lax.axis_size(axis)
    return lax.ppermute(x, axis, [(i, i ^ bit) for i in range(count)])


def bits_of(count):
    return [1 << k for k in range(count.bit_length() - 1)]


def ring_order(count):
    half = count // 2
    return [2 * p if p < half else 2 * (count - 1 - p) + 1 for p in range(count)]


def ring_slots(axis):
    count = lax.axis_size(axis)
    order = jnp.asarray(ring_order(count), jnp.int32)
    place = lax.axis_index(axis)
    spot = jnp.where(place % 2 == 0, place // 2, count - 1 - place // 2)
    steps = [0]
    for s in range(1, count // 2):
        steps += [-s, s]
    steps.append(count // 2)
    return order[jnp.mod(spot + jnp.asarray(steps, jnp.int32), count)]


def ring_step(r, l, axis):
    count = lax.axis_size(axis)
    order = ring_order(count)
    right = [(order[p], order[(p + 1) % count]) for p in range(count)]
    left = [(d, s) for s, d in right]
    return lax.ppermute(r, axis, right), lax.ppermute(l, axis, left)


def ring_last(r, l, axis):
    return ring_step(r[:1], l[1:], axis)


def across(w, axis):
    blocks = {0: w}
    for bit in bits_of(lax.axis_size(axis))[1:]:
        blocks |= {k ^ bit: swap(v, axis, bit) for k, v in list(blocks.items())}
    return blocks


def between(blocks, axis):
    return {k ^ 1: swap(v, axis, 1) for k, v in blocks.items()}


def in_order(blocks, axis):
    i = lax.axis_index(axis)
    count = lax.axis_size(axis)
    now = [blocks[k] for k in range(count)]
    for bit in bits_of(count):
        low = (i // bit) % 2 == 0
        now = [jnp.where(low, now[k], now[k ^ bit]) for k in range(count)]
    return jnp.concatenate(now, 0)


def added(keep, got):
    return (keep.astype(f32) + got.astype(f32)).astype(b16)


def core_parts(g):
    core = lax.axis_index("fsdp") % 2
    pairs = g.reshape((-1, 2) + g.shape[1:])
    send = lax.dynamic_index_in_dim(pairs, 1 - core, 1, keepdims=False)
    keep = lax.dynamic_index_in_dim(pairs, core, 1, keepdims=False)
    return send, keep


def chip_sum(x):
    bits = bits_of(lax.axis_size("fsdp"))[1:]
    for bit in bits[::-1]:
        upper = (lax.axis_index("fsdp") // bit) % 2
        pairs = x.reshape((2, -1) + x.shape[1:])
        send = lax.dynamic_index_in_dim(pairs, 1 - upper, 0, keepdims=False)
        keep = lax.dynamic_index_in_dim(pairs, upper, 0, keepdims=False)
        got = swap(send, "fsdp", bit)
        if bit != bits[0]:
            x = added(keep, got)
    return (keep, got), lambda keep, got: padded(added(keep, got)[0])


def padded(x):
    more = row_pad(x.shape[0], lax.axis_size("ctx"))
    return jnp.pad(x, ((0, more), (0, 0))) if more else x


def halve(x, axis, bit):
    upper = (lax.axis_index(axis) // bit) % 2
    half = x.shape[0] // 2
    send = lax.dynamic_slice_in_dim(x, (1 - upper) * half, half, 0)
    keep = lax.dynamic_slice_in_dim(x, upper * half, half, 0)
    return (keep, swap(send, axis, bit)), added


def unhalve(x, axis, bit):
    low = (lax.axis_index(axis) // bit) % 2 == 0

    def join(x, other):
        return jnp.concatenate([jnp.where(low, x, other), jnp.where(low, other, x)], 0)

    return (x, swap(x, axis, bit)), join


def block_sum_steps(blocks):
    bits = bits_of(blocks)
    down = [lambda x, bit=bit: halve(x, "ctx", bit) for bit in bits]
    up = [lambda x, bit=bit: unhalve(x, "ctx", bit) for bit in bits]
    return down + up[::-1]


def row_pad(rows, blocks):
    unit = 8 * blocks
    return -rows % unit


def dot_nt(a, b):
    return lax.dot_general(a, b, (((1,), (1,)), ((), ())), preferred_element_type=f32)


def dot_nn(a, b):
    return lax.dot_general(a, b, (((1,), (0,)), ((), ())), preferred_element_type=f32)


def lane_iota(rows):
    return lax.broadcasted_iota(jnp.int32, (rows, LANES), 1)


def split3(x):
    hi = x.astype(b16)
    rest = x - hi.astype(f32)
    mid = rest.astype(b16)
    low = (rest - mid.astype(f32)).astype(b16)
    return hi, mid, low


def place3(x, lane, at):
    hi, mid, low = (p.astype(f32) for p in split3(x))
    zero = jnp.zeros_like(x)
    return jnp.where(
        lane == at, hi, jnp.where(lane == at + 1, mid, jnp.where(lane == at + 2, low, zero))
    )


def stack_heads(pair):
    rows = pair.shape[0]
    lane = lane_iota(rows)
    zero = jnp.zeros_like(pair)
    return jnp.concatenate(
        [jnp.where(lane < HEAD_DIM, pair, zero), jnp.where(lane >= HEAD_DIM, pair, zero)], 0
    )


def join_heads(x):
    rows = x.shape[0] // 2
    return jnp.where(lane_iota(rows) < HEAD_DIM, x[:rows], x[rows:])


def key_extra(rows, base, length):
    lane = lane_iota(rows)
    dead = base + lax.broadcasted_iota(jnp.int32, (rows, LANES), 0) >= length
    mask = jnp.where(dead, MASKED, 0.0)
    return jnp.where(lane == MASK_LANE, mask, -1.0).astype(b16)


def spread_heads(x):
    rows = x.shape[0]
    lane = lane_iota(rows)
    other = pltpu.roll(x, HEAD_DIM, 1)
    return jnp.concatenate(
        [jnp.where(lane < HEAD_DIM, x, other), jnp.where(lane < HEAD_DIM, other, x)], 0
    )


def pair_columns(pair):
    return pl.ds(pl.multiple_of(pair * LANES, LANES), LANES)


def forward_kernel(slots, begin, final, bases, lengths, norms, q_ref, *refs):
    k_refs, v_refs = refs[:slots], refs[slots : 2 * slots]
    refs = refs[2 * slots :]
    if not begin:
        numer_in, sums_in, level_in = refs[:3]
        refs = refs[3:]
    if final:
        out_ref, extra_ref, meet_ref = refs
    else:
        numer_out, sums_out, level_out, meet_ref = refs
    seq = pl.program_id(0)
    length = lengths[seq]
    rows = q_ref.shape[1]
    block = k_refs[0].shape[1]
    pairs = q_ref.shape[2] // LANES
    lane2 = lane_iota(2 * rows)
    lane = lane_iota(rows)
    onehot = jnp.where(lane2 == MASK_LANE, 1.0, 0.0)
    for s in range(slots):
        meet_ref[s] = key_extra(block, bases[s], length)
    if final:
        extra_ref[0] = jnp.where(lane == MASK_LANE, 1.0, 0.0)

    def one_pair(leveled, pair, carry):
        cols = pair_columns(pair)
        stacked = stack_heads(q_ref[0, :, cols])
        lanes = onehot.astype(b16)
        now = jnp.zeros((rows, LANES), f32)
        if leveled:
            top = jnp.full((2 * rows, 1), MASKED, f32)
            probe = jnp.concatenate([stacked, lanes], 1)
            for s in range(slots):
                scores = dot_nt(probe, jnp.concatenate([k_refs[s][0, :, cols], meet_ref[s]], 1))
                top = jnp.maximum(top, jnp.max(scores, axis=1, keepdims=True))
            before = LOWEST if begin else spread_heads(level_in[0, :, cols])
            level = jnp.maximum(before, jnp.ceil(top * COEF))
            lanes = (place3(level / COEF, lane2, 0) + onehot).astype(b16)
            now = join_heads(jnp.broadcast_to(level, (2 * rows, LANES)))
        query = jnp.concatenate([stacked, lanes], 1)
        ones = jnp.ones((block, LANES), b16)
        total = jnp.zeros((2 * rows, 2 * LANES), f32)
        for s in range(slots):
            scores = dot_nt(query, jnp.concatenate([k_refs[s][0, :, cols], meet_ref[s]], 1))
            weights = jnp.exp2(scores * COEF).astype(b16)
            total = total + dot_nn(weights, jnp.concatenate([v_refs[s][0, :, cols], ones], 1))
        numer, sums = join_heads(total[:, :LANES]), join_heads(total[:, LANES:])
        if not begin:
            if leveled:
                factor = jnp.exp2(level_in[0, :, cols] - now)
                numer = numer + numer_in[0, :, cols] * factor
                sums = sums + sums_in[0, :, cols] * factor
            else:
                numer = numer + numer_in[0, :, cols]
                sums = sums + sums_in[0, :, cols]
        if not final:
            numer_out[0, :, cols] = numer
            sums_out[0, :, cols] = sums
            level_out[0, :, cols] = now
            return carry
        out_ref[0, :, cols] = numer / sums
        whole = spread_heads((now + jnp.log2(sums)) / COEF)
        extra_ref[0] += place3(whole[:rows], lane, 6 * pair) + place3(
            whole[rows:], lane, 6 * pair + 3
        )
        return carry

    most = jnp.float32(0.0)
    for head in range(2 * pairs):
        spot = seq * LANES + head
        most = jnp.maximum(most, norms[0, spot] * norms[1, spot])
    safe = most < (SAFE / COEF) ** 2

    @pl.when(safe)
    def _():
        lax.fori_loop(0, pairs, functools.partial(one_pair, False), 0, unroll=2)

    @pl.when(jnp.logical_not(safe))
    def _():
        lax.fori_loop(0, pairs, functools.partial(one_pair, True), 0)


def project_kernel(slots, w_ref, b_ref, *refs):
    x_refs, out_refs, norm_ref = refs[:slots], refs[slots : 2 * slots], refs[2 * slots]
    seqs, block, width = x_refs[0].shape
    cols = w_ref.shape[1]
    feature = lax.broadcasted_iota(jnp.int32, (cols, LANES), 0) // HEAD_DIM
    pick = jnp.where(feature == lax.broadcasted_iota(jnp.int32, (cols, LANES), 1), 1.0, 0.0)
    most = [jnp.zeros((1, LANES), f32)] * seqs
    for s in range(slots):
        x = x_refs[s][...].reshape(seqs * block, width)
        out = (dot_nn(x, w_ref[...]) + b_ref[...]).astype(b16)
        out_refs[s][...] = out.reshape(seqs, block, cols)

    @pl.when(pl.program_id(0) < 2)
    def _():
        for s in range(slots):
            wide = out_refs[s][...].reshape(seqs * block, cols).astype(f32)
            squares = dot_nn((wide * wide).astype(b16), pick.astype(b16))
            for k in range(seqs):
                here = jnp.max(squares[k * block : (k + 1) * block], axis=0, keepdims=True)
                most[k] = jnp.maximum(most[k], here)
        norm_ref[0] = jnp.concatenate(most, 1)


def project(xs, w, bias):
    slots = len(xs)
    seqs, block, width = xs[0].shape
    columns = w.shape[1]
    step = columns // 3
    whole = pl.BlockSpec((seqs, block, width), lambda j: (0, 0, 0))
    out = pl.pallas_call(
        functools.partial(project_kernel, slots),
        grid=(3,),
        in_specs=[
            pl.BlockSpec((width, step), lambda j: (0, j)),
            pl.BlockSpec((1, step), lambda j: (0, j)),
        ]
        + [whole] * slots,
        out_specs=[pl.BlockSpec((seqs, block, step), lambda j: (0, 0, j))] * slots
        + [pl.BlockSpec((1, 1, seqs * LANES), lambda j: (jnp.minimum(j, 1), 0, 0))],
        out_shape=[jax.ShapeDtypeStruct((seqs, block, columns), b16)] * slots
        + [jax.ShapeDtypeStruct((2, 1, seqs * LANES), f32)],
        compiler_params=pltpu.CompilerParams(vmem_limit_bytes=VMEM),
        cost_estimate=light(),
    )(w, bias, *xs)
    return list(out[:slots]), out[slots].reshape(2, seqs * LANES)


def gelu_kernel(x_ref, up_ref, bias_ref, down_ref, act_ref, slope_ref, branch_ref):
    pre = dot_nn(x_ref[...], up_ref[...]) + bias_ref[...]
    half = 0.5 + 0.5 * lax.erf(pre * math.sqrt(0.5))
    act = (pre * half).astype(b16)
    act_ref[...] = act
    bell = jnp.exp(pre * pre * -0.5) * (1.0 / math.sqrt(2.0 * math.pi))
    slope_ref[...] = (half + pre * bell).astype(b16)
    part = dot_nn(act, down_ref[...])

    @pl.when(pl.program_id(0) == 0)
    def _():
        branch_ref[...] = part

    @pl.when(pl.program_id(0) > 0)
    def _():
        branch_ref[...] += part


def feed_forward(x, up, bias, down):
    rows, width = x.shape
    units = up.shape[1]
    step = units // 3
    whole = pl.BlockSpec((rows, width), lambda j: (0, 0))
    wide = pl.BlockSpec((rows, step), lambda j: (0, j))
    return pl.pallas_call(
        gelu_kernel,
        grid=(3,),
        in_specs=[
            whole,
            pl.BlockSpec((width, step), lambda j: (0, j)),
            pl.BlockSpec((1, step), lambda j: (0, j)),
            pl.BlockSpec((step, width), lambda j: (j, 0)),
        ],
        out_specs=[wide, wide, whole],
        out_shape=[
            jax.ShapeDtypeStruct((rows, units), b16),
            jax.ShapeDtypeStruct((rows, units), b16),
            jax.ShapeDtypeStruct((rows, width), f32),
        ],
        compiler_params=pltpu.CompilerParams(vmem_limit_bytes=VMEM),
        cost_estimate=light(),
    )(x, up, bias, down)


def slope_kernel(grad_ref, down_ref, slope_ref, up_ref, start_ref, dpre_ref, sums_ref, out_ref):
    dact = dot_nt(grad_ref[...], down_ref[...])
    dpre = (slope_ref[...].astype(f32) * dact).astype(b16)
    dpre_ref[...] = dpre
    sums_ref[...] = jnp.sum(dpre.astype(f32), axis=0, keepdims=True)
    part = dot_nt(dpre, up_ref[...])

    @pl.when(pl.program_id(0) == 0)
    def _():
        out_ref[...] = start_ref[...] + part

    @pl.when(pl.program_id(0) > 0)
    def _():
        out_ref[...] += part


def feed_backward(grad, down, slope, up, start):
    rows, width = grad.shape
    units = up.shape[1]
    step = units // 3
    whole = pl.BlockSpec((rows, width), lambda j: (0, 0))
    wide = pl.BlockSpec((rows, step), lambda j: (0, j))
    return pl.pallas_call(
        slope_kernel,
        grid=(3,),
        in_specs=[
            whole,
            pl.BlockSpec((step, width), lambda j: (j, 0)),
            wide,
            pl.BlockSpec((width, step), lambda j: (0, j)),
            whole,
        ],
        out_specs=[wide, pl.BlockSpec((1, step), lambda j: (0, j)), whole],
        out_shape=[
            jax.ShapeDtypeStruct((rows, units), b16),
            jax.ShapeDtypeStruct((1, units), f32),
            jax.ShapeDtypeStruct((rows, width), f32),
        ],
        compiler_params=pltpu.CompilerParams(vmem_limit_bytes=VMEM),
        cost_estimate=light(),
    )(grad, down, slope, up, start)


def corr_kernel(grad_ref, value_ref, extra_ref, out_ref):
    width = grad_ref.shape[1]
    grad = grad_ref[...]
    feature = lax.broadcasted_iota(jnp.int32, (width, LANES), 0) // HEAD_DIM
    lane = lax.broadcasted_iota(jnp.int32, (width, LANES), 1)
    pick = jnp.where(
        (lane >= CORR_LANE) & (feature == (lane - CORR_LANE) // 3), 1.0, 0.0
    ).astype(b16)
    corr = sum(dot_nn(p, pick) for p in split3(grad * value_ref[...]))
    rows = grad.shape[0]
    lane = lane_iota(rows)
    hi, mid, low = (p.astype(f32) for p in split3(corr))
    part = lax.rem(lane, 3)
    placed = jnp.where(part == 0, hi, jnp.where(part == 1, mid, low))
    inside = (lane >= CORR_LANE) & (lane < CORR_LANE + 3 * (width // HEAD_DIM))
    out_ref[:, :width] = grad.astype(b16)
    out_ref[:, width:] = (extra_ref[...] + jnp.where(inside, placed, 0.0)).astype(b16)


def keep_lanes(x, lane, at):
    return jnp.where((lane >= at) & (lane < at + 3), x, jnp.zeros_like(x))


def query_kernel(slots, bases, lengths, q_ref, grad_ref, extra_ref, *refs):
    k_refs, v_refs = refs[:slots], refs[slots : 2 * slots]
    out_ref, meet_ref = refs[2 * slots :]
    seq = pl.program_id(0)
    length = lengths[seq]
    block = k_refs[0].shape[1]
    rows = q_ref.shape[1]
    lane = lane_iota(rows)
    onehot = jnp.where(lane == MASK_LANE, 1.0, 0.0).astype(b16)
    for s in range(slots):
        meet_ref[s] = key_extra(block, bases[s], length)

    def one_pair(pair, carry):
        cols = pair_columns(pair)
        extra = extra_ref[0]
        levels = [keep_lanes(extra, lane, 6 * pair + 3 * h) + onehot for h in range(2)]
        corrs = [keep_lanes(extra, lane, CORR_LANE + 6 * pair + 3 * h) for h in range(2)]
        query = jnp.concatenate([stack_heads(q_ref[0, :, cols]), jnp.concatenate(levels, 0)], 1)
        grad = jnp.concatenate([stack_heads(grad_ref[0, :, cols]), jnp.concatenate(corrs, 0)], 1)
        total = jnp.zeros((2 * rows, LANES), f32)
        for s in range(slots):
            meet = meet_ref[s]
            keys = k_refs[s][0, :, cols]
            weights = jnp.exp2(dot_nt(query, jnp.concatenate([keys, meet], 1)) * COEF)
            terms = dot_nt(grad, jnp.concatenate([v_refs[s][0, :, cols], meet], 1))
            total = total + dot_nn((weights * terms).astype(b16), keys)
        out_ref[0, :, cols] = (join_heads(total) * SCALE).astype(b16)
        return carry

    lax.fori_loop(0, q_ref.shape[2] // LANES, one_pair, 0, unroll=2)


def key_kernel(slots, begin, final, place, lengths, k_ref, v_ref, *refs):
    q_refs, g_refs, e_refs = refs[:slots], refs[slots : 2 * slots], refs[2 * slots : 3 * slots]
    refs = refs[3 * slots :]
    if not begin:
        dk_in, dv_in = refs[:2]
        refs = refs[2:]
    dk_ref, dv_ref = refs
    length = lengths[pl.program_id(0)]
    rows = k_ref.shape[1]
    lane = lane_iota(rows)
    dead = place[0] * rows + lax.broadcasted_iota(jnp.int32, (rows, LANES), 0) >= length
    mask = jnp.where((lane == MASK_LANE) & dead, MASKED, 0.0)
    minus = jnp.full((rows, LANES), -1.0, f32)

    def one_pair(pair, carry):
        cols = pair_columns(pair)
        levels = [(keep_lanes(minus, lane, 6 * pair + 3 * h) + mask).astype(b16) for h in range(2)]
        corrs = [
            keep_lanes(minus, lane, CORR_LANE + 6 * pair + 3 * h).astype(b16) for h in range(2)
        ]
        keys = jnp.concatenate([stack_heads(k_ref[0, :, cols]), jnp.concatenate(levels, 0)], 1)
        values = jnp.concatenate([stack_heads(v_ref[0, :, cols]), jnp.concatenate(corrs, 0)], 1)
        dkeys = jnp.zeros((2 * rows, LANES), f32)
        dvalues = jnp.zeros((2 * rows, LANES), f32)
        for s in range(slots):
            query, grad, extra = q_refs[s][0, :, cols], g_refs[s][0, :, cols], e_refs[s][0]
            weights = jnp.exp2(dot_nt(keys, jnp.concatenate([query, extra], 1)) * COEF)
            terms = dot_nt(values, jnp.concatenate([grad, extra], 1))
            dvalues = dvalues + dot_nn(weights.astype(b16), grad)
            dkeys = dkeys + dot_nn((weights * terms).astype(b16), query)
        dk, dv = join_heads(dkeys) * SCALE, join_heads(dvalues)
        if not begin:
            dk, dv = dk + dk_in[0, :, cols], dv + dv_in[0, :, cols]
        dk_ref[0, :, cols] = dk.astype(dk_ref.dtype)
        dv_ref[0, :, cols] = dv.astype(dv_ref.dtype)
        return carry

    lax.fori_loop(0, k_ref.shape[2] // LANES, one_pair, 0, unroll=2)


def third(block, width, which, seq_at=0):
    return pl.BlockSpec((1, block, width), lambda seq, *_: (seq_at + seq, 0, which))


def lanes_spec(block, at, seq_at=0):
    return pl.BlockSpec((1, block, LANES), lambda seq, *_: (seq_at + seq, 0, at))


def light():
    return pl.CostEstimate(flops=1000000, bytes_accessed=1000000, transcendentals=0)


def attend_forward(own, slots_qkv, bases, lengths, norms, state=(), final=False):
    slots = len(slots_qkv)
    seqs, block, triple = own.shape
    width = triple // 3
    q, k, v = (third(block, width, n) for n in range(3))
    part = jax.ShapeDtypeStruct((seqs, block, width), f32)
    if final:
        shapes = [part, jax.ShapeDtypeStruct((seqs, block, LANES), f32)]
        outs = [q, lanes_spec(block, 0)]
    else:
        shapes, outs = [part] * 3, [q] * 3
    return pl.pallas_call(
        functools.partial(forward_kernel, slots, not state, final),
        grid_spec=pltpu.PrefetchScalarGridSpec(
            num_scalar_prefetch=3,
            grid=(seqs,),
            in_specs=[q] + [k] * slots + [v] * slots + [q] * len(state),
            out_specs=outs,
            scratch_shapes=[pltpu.VMEM((slots, block, LANES), b16)],
        ),
        out_shape=shapes,
        compiler_params=pltpu.CompilerParams(vmem_limit_bytes=VMEM),
        cost_estimate=light(),
    )(bases, lengths, norms, own, *slots_qkv, *slots_qkv, *state)


def attend_query(seq_at, count, slots_qkv, grads, bases, lengths):
    slots = len(slots_qkv)
    block, triple = slots_qkv[0].shape[1:]
    width = triple // 3
    q, k, v = (third(block, width, n, seq_at) for n in range(3))
    return pl.pallas_call(
        functools.partial(query_kernel, slots),
        grid_spec=pltpu.PrefetchScalarGridSpec(
            num_scalar_prefetch=2,
            grid=(count,),
            in_specs=[q, q, lanes_spec(block, width // LANES, seq_at)]
            + [k] * slots
            + [v] * slots,
            out_specs=third(block, width, 0),
            scratch_shapes=[pltpu.VMEM((slots, block, LANES), b16)],
        ),
        out_shape=jax.ShapeDtypeStruct((count, block, width), b16),
        compiler_params=pltpu.CompilerParams(vmem_limit_bytes=VMEM_BACK),
        cost_estimate=light(),
    )(bases, lengths[seq_at : seq_at + count], slots_qkv[0], grads, grads, *slots_qkv, *slots_qkv)


def attend_keys(own, slots_qkv, slots_grads, place, lengths, state=(), final=False):
    slots = len(slots_qkv)
    seqs, block, triple = own.shape
    width = triple // 3
    q, k, v = (third(block, width, n) for n in range(3))
    shape = jax.ShapeDtypeStruct((seqs, block, width), b16 if final else f32)
    return pl.pallas_call(
        functools.partial(key_kernel, slots, not state, final),
        grid_spec=pltpu.PrefetchScalarGridSpec(
            num_scalar_prefetch=2,
            grid=(seqs,),
            in_specs=[k, v]
            + [q] * (2 * slots)
            + [lanes_spec(block, width // LANES)] * slots
            + [q] * len(state),
            out_specs=[q, q],
        ),
        out_shape=[shape, shape],
        compiler_params=pltpu.CompilerParams(vmem_limit_bytes=VMEM_BACK),
        cost_estimate=light(),
    )(place, lengths, own, own, *slots_qkv, *slots_grads, *slots_grads, *state)


def place_corr(dattended, attended, extra):
    rows, width = dattended.shape
    return pl.pallas_call(
        corr_kernel,
        out_shape=jax.ShapeDtypeStruct((rows, width + LANES), b16),
        compiler_params=pltpu.CompilerParams(vmem_limit_bytes=VMEM),
    )(dattended, attended, extra)


def layer_norm(value, gain, shift):
    mean = jnp.mean(value, axis=-1, keepdims=True)
    centred = value - mean
    spread = jnp.mean(centred * centred, axis=-1, keepdims=True)
    return centred * lax.rsqrt(spread + EPS) * gain + shift


def per_device(
    tokens,
    lengths,
    attend_weight,
    query_bias,
    value_bias,
    mixing_weight,
    mixing_bias,
    first_gain,
    first_shift,
    up_weight,
    up_bias,
    down_weight,
    down_bias,
    second_gain,
    second_shift,
    cotangent,
):
    seqs, block, width = tokens.shape
    rows = seqs * block
    owners = lax.axis_size("fsdp")
    blocks = lax.axis_size("ctx")
    place = lax.axis_index("ctx")
    share = width // owners
    steps = blocks // 2

    flat = tokens.reshape(rows, width)
    flat_low = flat.astype(b16)
    own_tokens = flat_low.reshape(seqs, block, width)
    own_tokens, attend_weight, mixing_weight = together(own_tokens, attend_weight, mixing_weight)

    spots = ring_slots("ctx")
    bases = spots * block

    def pick(blocks_at):
        keys = list(blocks_at)
        return keys, [blocks_at[k] for k in keys]

    def complete(got, near):
        blocks_at = dict(zip(keys, got))
        far = between({k: v for k, v in blocks_at.items() if k}, "fsdp")
        return blocks_at | far | {1: near}

    tr, tl = ring_step(own_tokens, own_tokens, "ctx")
    keys, attend_got = pick(across(attend_weight, "fsdp"))
    small = jnp.concatenate(
        [query_bias, value_bias, mixing_bias, first_gain, first_shift, down_bias,
         second_gain, second_shift, up_bias]
    )
    small_rows = -(-small.shape[0] // (16 * LANES)) * 16
    small = jnp.pad(small, (0, small_rows * LANES - small.shape[0])).reshape(small_rows, LANES)
    small_blocks = across(small, "fsdp")
    small_full = in_order(small_blocks | between(small_blocks, "fsdp"), "fsdp")
    attend_near = between({0: attend_weight}, "fsdp")[1]
    tr, tl, mixing_weight, up_weight, small_full, attend_near, *attend_got = together(
        tr, tl, mixing_weight, up_weight, small_full, attend_near, *attend_got
    )
    token_slots = [own_tokens, tr, tl]

    tr, tl = ring_step(tr, tl, "ctx")
    attend_blocks = complete(attend_got, attend_near)
    _, mixing_got = pick(across(mixing_weight, "fsdp"))
    _, up_got = pick(across(up_weight, "fsdp"))
    small_full = small_full.reshape(owners, -1).astype(f32)
    vectors = small_full[:, : 8 * share].reshape(owners, 8, share).transpose(1, 0, 2)
    vectors = vectors.reshape(8, width)
    qbias, vbias, mixbias, fgain, fshift, downbias, sgain, sshift = (
        vectors[k : k + 1] for k in range(8)
    )
    upbias = small_full[:, 8 * share : 8 * share + up_bias.shape[0]].reshape(1, -1)
    bias = jnp.concatenate([qbias, jnp.zeros_like(qbias), vbias], 1)
    attend_full = in_order(attend_blocks, "fsdp")
    slots_qkv, norms = project(token_slots, attend_full, bias)
    mixing_near = between({0: mixing_weight}, "fsdp")[1]
    up_near = between({0: up_weight}, "fsdp")[1]
    tr, tl, down_weight, mixing_near, up_near, *rest = together(
        tr, tl, down_weight, mixing_near, up_near, *mixing_got, *slots_qkv
    )
    mixing_got, slots_qkv = rest[: len(keys)], rest[len(keys) :]
    token_slots += [tr, tl]

    state = ()
    used = 0
    for step in range(3, steps + 1):
        last = step == steps
        nr, nl = ring_last(tr, tl, "ctx") if last else ring_step(tr, tl, "ctx")
        fresh, more = project(token_slots[len(slots_qkv) :], attend_full, bias)
        slots_qkv += fresh
        norms = jnp.maximum(norms, more)
        if step == 3:
            _, down_got = pick(across(down_weight, "fsdp"))
            down_near = between({0: down_weight}, "fsdp")[1]
            mixing_full = in_order(complete(mixing_got, mixing_near), "fsdp")
        if last:
            up_blocks = complete(up_got, up_near)
            tr, tl, *slots_qkv = together(nr, nl, *slots_qkv)
            token_slots.append(jnp.concatenate([tr, tl], 0))
        else:
            use = slice(used, len(slots_qkv))
            state = attend_forward(
                slots_qkv[0], slots_qkv[use], bases[use], lengths, norms, tuple(state)
            )
            used = len(slots_qkv)
            tr, tl, mixing_full, *rest = together(nr, nl, mixing_full, *up_got, *state)
            up_got, state = rest[: len(keys)], rest[len(keys) :]
            token_slots += [tr, tl]
    fresh, more = project(token_slots[len(slots_qkv) :], attend_full, bias)
    slots_qkv += fresh
    norms = jnp.maximum(norms, more)
    attended3, extra = attend_forward(
        slots_qkv[0], slots_qkv[used:], bases[used:], lengths, norms, tuple(state), True
    )
    up_full = in_order(up_blocks, "fsdp")
    down_full = in_order(complete(down_got, down_near), "fsdp")

    attended = attended3.reshape(rows, width)
    attended_low = attended.astype(b16)
    mixed = jnp.dot(attended_low, mixing_full, preferred_element_type=f32) + mixbias
    hidden = flat + mixed
    first, first_back = jax.vjp(layer_norm, hidden, fgain, fshift)
    first_low = first.astype(b16)
    act_low, slope, branch = feed_forward(first_low, up_full, upbias, down_full)
    summed = first + branch + downbias
    result, second_back = jax.vjp(layer_norm, summed, sgain, sshift)
    dsummed, grad_sgain, grad_sshift = second_back(cotangent.reshape(rows, width))
    dbranch = dsummed.astype(b16)
    grad_down = jnp.einsum("rf,rd->fd", act_low, dbranch, preferred_element_type=f32).astype(b16)
    down_send, down_keep = core_parts(grad_down.reshape(owners, -1, width))
    down_got = swap(down_send, "fsdp", 1)
    dpre, grad_upbias, dfirst = feed_backward(dbranch, down_full, slope, up_full, dsummed)
    dpre, dfirst, down_got = together(dpre, dfirst, down_got)
    grad_up = jnp.einsum("rd,rf->df", first_low, dpre, preferred_element_type=f32).astype(b16)
    up_send, up_keep = core_parts(grad_up.reshape(owners, share, -1))
    up_got = swap(up_send, "fsdp", 1)
    way_down, end_down = chip_sum(added(down_keep, down_got))
    dhidden, grad_fgain, grad_fshift = first_back(dfirst)
    dmixed = dhidden.astype(b16)
    dattended = jnp.einsum("re,de->rd", dmixed, mixing_full, preferred_element_type=f32)

    grads = place_corr(dattended, attended, extra.reshape(rows, LANES))
    grads = grads.reshape(seqs, block, width + LANES)
    grads, attended_low, dmixed, up_got = together(grads, attended_low, dmixed, up_got)

    def summed_rows(x):
        return jnp.sum(x.astype(f32), axis=0)

    steps_ctx = block_sum_steps(blocks)
    place1 = place.reshape(1)

    gr, gl = ring_step(grads, grads, "ctx")
    way_up, end_up = chip_sum(added(up_keep, up_got))
    dquery = [attend_query(0, 1, slots_qkv, grads, bases, lengths)]
    gr, gl, grads, dquery[0], dmixed, *way_down = together(
        gr, gl, grads, dquery[0], dmixed, *way_down
    )
    grad_slots = [grads, gr, gl]

    gr, gl = ring_step(gr, gl, "ctx")
    way_down, end_down = steps_ctx[0](end_down(*way_down))
    grad_mixing = jnp.einsum("rd,re->de", attended_low, dmixed, preferred_element_type=f32)
    dquery.append(attend_query(1, 1, slots_qkv, grads, bases, lengths))
    gr, gl, grad_mixing, dquery[1], *ways = together(
        gr, gl, grad_mixing, dquery[1], *way_down, *way_up
    )
    way_down, way_up = ways[:2], ways[2:]
    grad_slots += [gr, gl]
    dquery = jnp.concatenate(dquery, 0).reshape(rows, width)

    vectors = [
        summed_rows(dmixed), grad_fgain, grad_fshift, summed_rows(dbranch), grad_sgain,
        grad_sshift, grad_upbias, summed_rows(dquery),
    ]
    vectors = jnp.concatenate([v.reshape(owners, -1) for v in vectors], 1)
    need = -(-vectors.shape[1] // width)
    need += row_pad(need + 2 * share, blocks)
    vectors = jnp.pad(vectors, ((0, 0), (0, need * width - vectors.shape[1])))
    vectors = vectors.astype(b16).reshape(owners, need, width)
    dkv = ()
    used = 0
    for step in range(3, steps + 1):
        last = step == steps
        nr, nl = ring_last(gr, gl, "ctx") if last else ring_step(gr, gl, "ctx")
        if step == 3:
            grad_query = jnp.einsum("rd,re->de", flat_low, dquery, preferred_element_type=f32)
            mixed_parts = jnp.concatenate(
                [
                    grad_mixing.astype(b16).reshape(owners, share, width),
                    grad_query.astype(b16).reshape(owners, share, width),
                    vectors,
                ],
                1,
            )
            third_send, third_keep = core_parts(mixed_parts)
            third_got = swap(third_send, "fsdp", 1)
            way_down, end_down = steps_ctx[1](end_down(*way_down))
            way_up, end_up = steps_ctx[0](end_up(*way_up))
        if last:
            way_third, end_third = chip_sum(added(third_keep, third_got))
            way_down, end_down = steps_ctx[2](end_down(*way_down))
            way_up, end_up = steps_ctx[1](end_up(*way_up))
        use = slice(used, len(grad_slots) - (0 if last else 2))
        dkv = attend_keys(
            slots_qkv[0], slots_qkv[use], grad_slots[use], place1, lengths, tuple(dkv)
        )
        used = use.stop
        gr, gl, dkv0, dkv1, third_got, *ways = together(
            nr, nl, *dkv, third_got, *way_down, *way_up
        )
        way_down, way_up = ways[:2], ways[2:]
        dkv = (dkv0, dkv1)
        grad_slots += [jnp.concatenate([gr, gl], 0)] if last else [gr, gl]

    way_down, end_down = steps_ctx[3](end_down(*way_down))
    way_up, end_up = steps_ctx[2](end_up(*way_up))
    dkeys, dvalues = attend_keys(
        slots_qkv[0], slots_qkv[used:], grad_slots[used:], place1, lengths, tuple(dkv), True
    )
    dkeys, dvalues, *ways = together(dkeys, dvalues, *way_down, *way_up, *way_third)
    way_down, way_up, way_third = ways[:2], ways[2:4], ways[4:]
    dkeys, dvalues = dkeys.reshape(rows, width), dvalues.reshape(rows, width)
    dlate = jnp.concatenate([dkeys, dvalues], 1)
    tokens_across = flat_low.T

    core = lax.axis_index("fsdp") % 2
    first_column = (jnp.arange(LANES) == 0).astype(b16)
    bias_columns = jnp.broadcast_to(first_column, (rows, LANES))
    vector = jnp.einsum("rd,re->de", dvalues, bias_columns, preferred_element_type=f32)
    vector = vector.reshape(owners // 2, 2, share, LANES)

    def late_part(which):
        mine = lax.dynamic_index_in_dim(
            tokens_across.reshape(owners // 2, 2, share, rows), which, 1, keepdims=False
        )
        main = jnp.einsum("osr,re->ose", mine, dlate, preferred_element_type=f32)
        extra_columns = lax.dynamic_index_in_dim(vector, which, 1, keepdims=False)
        return jnp.concatenate([main, extra_columns], 2).astype(b16)

    late_got = swap(late_part(1 - core), "fsdp", 1)
    late_keep = late_part(core)
    dprojected = jnp.concatenate([dquery, dlate], 1)

    tokens_grad = dhidden + jnp.einsum(
        "re,de->rd", dprojected, attend_full, preferred_element_type=f32
    )

    chains = [
        (way_down, end_down, steps_ctx[4:]),
        (way_up, end_up, steps_ctx[3:]),
        (way_third, end_third, steps_ctx),
        ((late_keep, late_got), added, [chip_sum] + steps_ctx),
    ]
    sums = [None] * len(chains)
    begin = True
    while any(chains):
        active = [k for k, chain in enumerate(chains) if chain]
        for k in active:
            way, end, left = chains[k]
            if begin and k == 3:
                continue
            value = end(*way)
            if left:
                chains[k] = (*left[0](value), left[1:])
            else:
                sums[k], chains[k] = value, None
        active = [k for k, chain in enumerate(chains) if chain]
        ways = [tuple(chains[k][0]) for k in active]
        if begin:
            ways, tokens_grad = together(ways, tokens_grad)
        elif active:
            (ways,) = together(ways)
        for k, way in zip(active, ways):
            chains[k] = (way,) + chains[k][1:]
        begin = False
    one, two, three, four = (v.astype(f32) for v in sums)

    own_down = one[: down_weight.shape[0]]
    own_up = two[:share]
    own_mixing = three[:share]
    own_attend = jnp.concatenate([three[share : 2 * share], four[:share, : 2 * width]], 1)
    own_vbias = four[:share, 2 * width]
    vectors = three[2 * share : 2 * share + need].reshape(-1)
    own_mixbias, own_fgain, own_fshift, own_downbias, own_sgain, own_sshift = (
        vectors[k * share : (k + 1) * share] for k in range(6)
    )
    at = 6 * share + up_bias.shape[0]
    own_upbias = vectors[6 * share : at]
    own_qbias = vectors[at : at + share]
    return (
        result.reshape(seqs, block, width),
        tokens_grad.reshape(seqs, block, width),
        own_attend,
        own_qbias,
        own_vbias,
        own_mixing,
        own_mixbias,
        own_fgain,
        own_fshift,
        own_up,
        own_upbias,
        own_down,
        own_downbias,
        own_sgain,
        own_sshift,
    )


def solution(mesh):
    rows = P("fsdp", "ctx", None)
    matrix = P("fsdp", None)
    vector = P("fsdp")
    return jax.shard_map(
        per_device,
        mesh=mesh,
        in_specs=(
            rows, vector, matrix, vector, vector, matrix, vector, vector, vector,
            matrix, vector, matrix, vector, vector, vector, rows,
        ),
        out_specs=(
            rows, rows, matrix, vector, vector, matrix, vector, vector, vector,
            matrix, vector, matrix, vector, vector, vector,
        ),
        check_vma=False,
    )
```

```python
import functools
import math

import jax
import jax.numpy as jnp
from jax import lax
from jax.experimental import pallas as pl
from jax.experimental.pallas import tpu as pltpu
from jax.sharding import PartitionSpec as P

HEAD_DIM = 64
LANES = 128
EPS = 1e-12
SCALE = 0.125
LOG2E = math.log2(math.e)
COEF = SCALE * LOG2E
MASKED = -1e30
SAFE = 60.0
LOWEST = -1e9
MASK_LANE = 127
CORR_LANE = 36
VMEM = 30 * 1024 * 1024
VMEM_BACK = 52 * 1024 * 1024

f32 = jnp.float32
b16 = jnp.bfloat16


def together(*values):
    return lax.optimization_barrier(values)


def swap(x, axis, bit):
    count = lax.axis_size(axis)
    return lax.ppermute(x, axis, [(i, i ^ bit) for i in range(count)])


def bits_of(count):
    return [1 << k for k in range(count.bit_length() - 1)]


def ring_order(count):
    half = count // 2
    return [2 * p if p < half else 2 * (count - 1 - p) + 1 for p in range(count)]


def ring_slots(axis):
    count = lax.axis_size(axis)
    order = jnp.asarray(ring_order(count), jnp.int32)
    place = lax.axis_index(axis)
    spot = jnp.where(place % 2 == 0, place // 2, count - 1 - place // 2)
    steps = [0]
    for s in range(1, count // 2):
        steps += [-s, s]
    steps.append(count // 2)
    return order[jnp.mod(spot + jnp.asarray(steps, jnp.int32), count)]


def ring_step(r, l, axis):
    count = lax.axis_size(axis)
    order = ring_order(count)
    right = [(order[p], order[(p + 1) % count]) for p in range(count)]
    left = [(d, s) for s, d in right]
    return lax.ppermute(r, axis, right), lax.ppermute(l, axis, left)


def ring_last(r, l, axis):
    return ring_step(r[:1], l[1:], axis)


def across(w, axis):
    blocks = {0: w}
    for bit in bits_of(lax.axis_size(axis))[1:]:
        blocks |= {k ^ bit: swap(v, axis, bit) for k, v in list(blocks.items())}
    return blocks


def between(blocks, axis):
    return {k ^ 1: swap(v, axis, 1) for k, v in blocks.items()}


def in_order(blocks, axis):
    i = lax.axis_index(axis)
    count = lax.axis_size(axis)
    now = [blocks[k] for k in range(count)]
    for bit in bits_of(count):
        low = (i // bit) % 2 == 0
        now = [jnp.where(low, now[k], now[k ^ bit]) for k in range(count)]
    return jnp.concatenate(now, 0)


def added(keep, got):
    return (keep.astype(f32) + got.astype(f32)).astype(b16)


def core_parts(g):
    core = lax.axis_index("fsdp") % 2
    pairs = g.reshape((-1, 2) + g.shape[1:])
    send = lax.dynamic_index_in_dim(pairs, 1 - core, 1, keepdims=False)
    keep = lax.dynamic_index_in_dim(pairs, core, 1, keepdims=False)
    return send, keep


def chip_sum(x):
    bits = bits_of(lax.axis_size("fsdp"))[1:]
    for bit in bits[::-1]:
        upper = (lax.axis_index("fsdp") // bit) % 2
        pairs = x.reshape((2, -1) + x.shape[1:])
        send = lax.dynamic_index_in_dim(pairs, 1 - upper, 0, keepdims=False)
        keep = lax.dynamic_index_in_dim(pairs, upper, 0, keepdims=False)
        got = swap(send, "fsdp", bit)
        if bit != bits[0]:
            x = added(keep, got)
    return (keep, got), lambda keep, got: padded(added(keep, got)[0])


def padded(x):
    more = row_pad(x.shape[0], lax.axis_size("ctx"))
    return jnp.pad(x, ((0, more), (0, 0))) if more else x


def halve(x, axis, bit):
    upper = (lax.axis_index(axis) // bit) % 2
    half = x.shape[0] // 2
    send = lax.dynamic_slice_in_dim(x, (1 - upper) * half, half, 0)
    keep = lax.dynamic_slice_in_dim(x, upper * half, half, 0)
    return (keep, swap(send, axis, bit)), added


def unhalve(x, axis, bit):
    low = (lax.axis_index(axis) // bit) % 2 == 0

    def join(x, other):
        return jnp.concatenate([jnp.where(low, x, other), jnp.where(low, other, x)], 0)

    return (x, swap(x, axis, bit)), join


def block_sum_steps(blocks, order):
    bits = bits_of(blocks)
    bits = bits[:2][:: -1 if order else 1] + bits[2:]
    down = [lambda x, bit=bit: halve(x, "ctx", bit) for bit in bits]
    up = [lambda x, bit=bit: unhalve(x, "ctx", bit) for bit in bits]
    return down + up[::-1]


def row_pad(rows, blocks):
    unit = 8 * blocks
    return -rows % unit


def dot_nt(a, b):
    return lax.dot_general(a, b, (((1,), (1,)), ((), ())), preferred_element_type=f32)


def dot_nn(a, b):
    return lax.dot_general(a, b, (((1,), (0,)), ((), ())), preferred_element_type=f32)


def lane_iota(rows):
    return lax.broadcasted_iota(jnp.int32, (rows, LANES), 1)


def split3(x):
    hi = x.astype(b16)
    rest = x - hi.astype(f32)
    mid = rest.astype(b16)
    low = (rest - mid.astype(f32)).astype(b16)
    return hi, mid, low


def place3(x, lane, at):
    hi, mid, low = (p.astype(f32) for p in split3(x))
    zero = jnp.zeros_like(x)
    return jnp.where(
        lane == at, hi, jnp.where(lane == at + 1, mid, jnp.where(lane == at + 2, low, zero))
    )


def stack_heads(pair):
    rows = pair.shape[0]
    lane = lane_iota(rows)
    zero = jnp.zeros_like(pair)
    return jnp.concatenate(
        [jnp.where(lane < HEAD_DIM, pair, zero), jnp.where(lane >= HEAD_DIM, pair, zero)], 0
    )


def join_heads(x):
    rows = x.shape[0] // 2
    return jnp.where(lane_iota(rows) < HEAD_DIM, x[:rows], x[rows:])


def key_extra(rows, base, length):
    lane = lane_iota(rows)
    dead = base + lax.broadcasted_iota(jnp.int32, (rows, LANES), 0) >= length
    mask = jnp.where(dead, MASKED, 0.0)
    return jnp.where(lane == MASK_LANE, mask, -1.0).astype(b16)


def spread_heads(x):
    rows = x.shape[0]
    lane = lane_iota(rows)
    other = pltpu.roll(x, HEAD_DIM, 1)
    return jnp.concatenate(
        [jnp.where(lane < HEAD_DIM, x, other), jnp.where(lane < HEAD_DIM, other, x)], 0
    )


def pair_columns(pair):
    return pl.ds(pl.multiple_of(pair * LANES, LANES), LANES)


def forward_kernel(slots, begin, final, bases, lengths, norms, q_ref, *refs):
    k_refs, v_refs = refs[:slots], refs[slots : 2 * slots]
    refs = refs[2 * slots :]
    if not begin:
        numer_in, sums_in, level_in = refs[:3]
        refs = refs[3:]
    if final:
        out_ref, extra_ref, meet_ref = refs
    else:
        numer_out, sums_out, level_out, meet_ref = refs
    seq = pl.program_id(0)
    length = lengths[seq]
    rows = q_ref.shape[1]
    block = k_refs[0].shape[1]
    pairs = q_ref.shape[2] // LANES
    lane2 = lane_iota(2 * rows)
    lane = lane_iota(rows)
    onehot = jnp.where(lane2 == MASK_LANE, 1.0, 0.0)
    for s in range(slots):
        meet_ref[s] = key_extra(block, bases[s], length)
    if final:
        extra_ref[0] = jnp.where(lane == MASK_LANE, 1.0, 0.0)

    def one_pair(leveled, pair, carry):
        cols = pair_columns(pair)
        stacked = stack_heads(q_ref[0, :, cols])
        lanes = onehot.astype(b16)
        now = jnp.zeros((rows, LANES), f32)
        if leveled:
            top = jnp.full((2 * rows, 1), MASKED, f32)
            probe = jnp.concatenate([stacked, lanes], 1)
            for s in range(slots):
                scores = dot_nt(probe, jnp.concatenate([k_refs[s][0, :, cols], meet_ref[s]], 1))
                top = jnp.maximum(top, jnp.max(scores, axis=1, keepdims=True))
            before = LOWEST if begin else spread_heads(level_in[0, :, cols])
            level = jnp.maximum(before, jnp.ceil(top * COEF))
            lanes = (place3(level / COEF, lane2, 0) + onehot).astype(b16)
            now = join_heads(jnp.broadcast_to(level, (2 * rows, LANES)))
        query = jnp.concatenate([stacked, lanes], 1)
        ones = jnp.ones((block, LANES), b16)
        total = jnp.zeros((2 * rows, 2 * LANES), f32)
        for s in range(slots):
            scores = dot_nt(query, jnp.concatenate([k_refs[s][0, :, cols], meet_ref[s]], 1))
            weights = jnp.exp2(scores * COEF).astype(b16)
            total = total + dot_nn(weights, jnp.concatenate([v_refs[s][0, :, cols], ones], 1))
        numer, sums = join_heads(total[:, :LANES]), join_heads(total[:, LANES:])
        if not begin:
            if leveled:
                factor = jnp.exp2(level_in[0, :, cols] - now)
                numer = numer + numer_in[0, :, cols] * factor
                sums = sums + sums_in[0, :, cols] * factor
            else:
                numer = numer + numer_in[0, :, cols]
                sums = sums + sums_in[0, :, cols]
        if not final:
            numer_out[0, :, cols] = numer
            sums_out[0, :, cols] = sums
            level_out[0, :, cols] = now
            return carry
        out_ref[0, :, cols] = numer / sums
        whole = spread_heads((now + jnp.log2(sums)) / COEF)
        extra_ref[0] += place3(whole[:rows], lane, 6 * pair) + place3(
            whole[rows:], lane, 6 * pair + 3
        )
        return carry

    most = jnp.float32(0.0)
    for head in range(2 * pairs):
        spot = seq * LANES + head
        most = jnp.maximum(most, norms[0, spot] * norms[1, spot])
    safe = most < (SAFE / COEF) ** 2

    @pl.when(safe)
    def _():
        lax.fori_loop(0, pairs, functools.partial(one_pair, False), 0, unroll=2)

    @pl.when(jnp.logical_not(safe))
    def _():
        lax.fori_loop(0, pairs, functools.partial(one_pair, True), 0)


def project_kernel(slots, w_ref, b_ref, *refs):
    x_refs, out_refs, norm_ref = refs[:slots], refs[slots : 2 * slots], refs[2 * slots]
    seqs, block, width = x_refs[0].shape
    cols = w_ref.shape[1]
    feature = lax.broadcasted_iota(jnp.int32, (cols, LANES), 0) // HEAD_DIM
    pick = jnp.where(feature == lax.broadcasted_iota(jnp.int32, (cols, LANES), 1), 1.0, 0.0)
    most = [jnp.zeros((1, LANES), f32)] * seqs
    for s in range(slots):
        x = x_refs[s][...].reshape(seqs * block, width)
        out = (dot_nn(x, w_ref[...]) + b_ref[...]).astype(b16)
        out_refs[s][...] = out.reshape(seqs, block, cols)

    @pl.when(pl.program_id(0) < 2)
    def _():
        for s in range(slots):
            wide = out_refs[s][...].reshape(seqs * block, cols).astype(f32)
            squares = dot_nn((wide * wide).astype(b16), pick.astype(b16))
            for k in range(seqs):
                here = jnp.max(squares[k * block : (k + 1) * block], axis=0, keepdims=True)
                most[k] = jnp.maximum(most[k], here)
        norm_ref[0] = jnp.concatenate(most, 1)


def project(xs, w, bias):
    slots = len(xs)
    seqs, block, width = xs[0].shape
    columns = w.shape[1]
    step = columns // 3
    whole = pl.BlockSpec((seqs, block, width), lambda j: (0, 0, 0))
    out = pl.pallas_call(
        functools.partial(project_kernel, slots),
        grid=(3,),
        in_specs=[
            pl.BlockSpec((width, step), lambda j: (0, j)),
            pl.BlockSpec((1, step), lambda j: (0, j)),
        ]
        + [whole] * slots,
        out_specs=[pl.BlockSpec((seqs, block, step), lambda j: (0, 0, j))] * slots
        + [pl.BlockSpec((1, 1, seqs * LANES), lambda j: (jnp.minimum(j, 1), 0, 0))],
        out_shape=[jax.ShapeDtypeStruct((seqs, block, columns), b16)] * slots
        + [jax.ShapeDtypeStruct((2, 1, seqs * LANES), f32)],
        compiler_params=pltpu.CompilerParams(vmem_limit_bytes=VMEM),
        cost_estimate=light(),
    )(w, bias, *xs)
    return list(out[:slots]), out[slots].reshape(2, seqs * LANES)


def gelu_kernel(x_ref, up_ref, bias_ref, down_ref, act_ref, slope_ref, branch_ref):
    pre = dot_nn(x_ref[...], up_ref[...]) + bias_ref[...]
    half = 0.5 + 0.5 * lax.erf(pre * math.sqrt(0.5))
    act = (pre * half).astype(b16)
    act_ref[...] = act
    bell = jnp.exp(pre * pre * -0.5) * (1.0 / math.sqrt(2.0 * math.pi))
    slope_ref[...] = (half + pre * bell).astype(b16)
    part = dot_nn(act, down_ref[...])

    @pl.when(pl.program_id(0) == 0)
    def _():
        branch_ref[...] = part

    @pl.when(pl.program_id(0) > 0)
    def _():
        branch_ref[...] += part


def feed_forward(x, up, bias, down):
    rows, width = x.shape
    units = up.shape[1]
    step = units // 3
    whole = pl.BlockSpec((rows, width), lambda j: (0, 0))
    wide = pl.BlockSpec((rows, step), lambda j: (0, j))
    return pl.pallas_call(
        gelu_kernel,
        grid=(3,),
        in_specs=[
            whole,
            pl.BlockSpec((width, step), lambda j: (0, j)),
            pl.BlockSpec((1, step), lambda j: (0, j)),
            pl.BlockSpec((step, width), lambda j: (j, 0)),
        ],
        out_specs=[wide, wide, whole],
        out_shape=[
            jax.ShapeDtypeStruct((rows, units), b16),
            jax.ShapeDtypeStruct((rows, units), b16),
            jax.ShapeDtypeStruct((rows, width), f32),
        ],
        compiler_params=pltpu.CompilerParams(vmem_limit_bytes=VMEM),
        cost_estimate=light(),
    )(x, up, bias, down)


def slope_kernel(grad_ref, down_ref, slope_ref, up_ref, start_ref, dpre_ref, sums_ref, out_ref):
    dact = dot_nt(grad_ref[...], down_ref[...])
    dpre = (slope_ref[...].astype(f32) * dact).astype(b16)
    dpre_ref[...] = dpre
    sums_ref[...] = jnp.sum(dpre.astype(f32), axis=0, keepdims=True)
    part = dot_nt(dpre, up_ref[...])

    @pl.when(pl.program_id(0) == 0)
    def _():
        out_ref[...] = start_ref[...] + part

    @pl.when(pl.program_id(0) > 0)
    def _():
        out_ref[...] += part


def feed_backward(grad, down, slope, up, start):
    rows, width = grad.shape
    units = up.shape[1]
    step = units // 3
    whole = pl.BlockSpec((rows, width), lambda j: (0, 0))
    wide = pl.BlockSpec((rows, step), lambda j: (0, j))
    return pl.pallas_call(
        slope_kernel,
        grid=(3,),
        in_specs=[
            whole,
            pl.BlockSpec((step, width), lambda j: (j, 0)),
            wide,
            pl.BlockSpec((width, step), lambda j: (0, j)),
            whole,
        ],
        out_specs=[wide, pl.BlockSpec((1, step), lambda j: (0, j)), whole],
        out_shape=[
            jax.ShapeDtypeStruct((rows, units), b16),
            jax.ShapeDtypeStruct((1, units), f32),
            jax.ShapeDtypeStruct((rows, width), f32),
        ],
        compiler_params=pltpu.CompilerParams(vmem_limit_bytes=VMEM),
        cost_estimate=light(),
    )(grad, down, slope, up, start)


def corr_kernel(grad_ref, value_ref, extra_ref, out_ref):
    width = grad_ref.shape[1]
    grad = grad_ref[...]
    feature = lax.broadcasted_iota(jnp.int32, (width, LANES), 0) // HEAD_DIM
    lane = lax.broadcasted_iota(jnp.int32, (width, LANES), 1)
    pick = jnp.where(
        (lane >= CORR_LANE) & (feature == (lane - CORR_LANE) // 3), 1.0, 0.0
    ).astype(b16)
    corr = sum(dot_nn(p, pick) for p in split3(grad * value_ref[...]))
    rows = grad.shape[0]
    lane = lane_iota(rows)
    hi, mid, low = (p.astype(f32) for p in split3(corr))
    part = lax.rem(lane, 3)
    placed = jnp.where(part == 0, hi, jnp.where(part == 1, mid, low))
    inside = (lane >= CORR_LANE) & (lane < CORR_LANE + 3 * (width // HEAD_DIM))
    out_ref[:, :width] = grad.astype(b16)
    out_ref[:, width:] = (extra_ref[...] + jnp.where(inside, placed, 0.0)).astype(b16)


def keep_lanes(x, lane, at):
    return jnp.where((lane >= at) & (lane < at + 3), x, jnp.zeros_like(x))


def query_kernel(slots, bases, lengths, q_ref, grad_ref, extra_ref, *refs):
    k_refs, v_refs = refs[:slots], refs[slots : 2 * slots]
    out_ref, meet_ref = refs[2 * slots :]
    seq = pl.program_id(0)
    length = lengths[seq]
    block = k_refs[0].shape[1]
    rows = q_ref.shape[1]
    lane = lane_iota(rows)
    onehot = jnp.where(lane == MASK_LANE, 1.0, 0.0).astype(b16)
    for s in range(slots):
        meet_ref[s] = key_extra(block, bases[s], length)

    def one_pair(pair, carry):
        cols = pair_columns(pair)
        extra = extra_ref[0]
        levels = [keep_lanes(extra, lane, 6 * pair + 3 * h) + onehot for h in range(2)]
        corrs = [keep_lanes(extra, lane, CORR_LANE + 6 * pair + 3 * h) for h in range(2)]
        query = jnp.concatenate([stack_heads(q_ref[0, :, cols]), jnp.concatenate(levels, 0)], 1)
        grad = jnp.concatenate([stack_heads(grad_ref[0, :, cols]), jnp.concatenate(corrs, 0)], 1)
        total = jnp.zeros((2 * rows, LANES), f32)
        for s in range(slots):
            meet = meet_ref[s]
            keys = k_refs[s][0, :, cols]
            weights = jnp.exp2(dot_nt(query, jnp.concatenate([keys, meet], 1)) * COEF)
            terms = dot_nt(grad, jnp.concatenate([v_refs[s][0, :, cols], meet], 1))
            total = total + dot_nn((weights * terms).astype(b16), keys)
        out_ref[0, :, cols] = (join_heads(total) * SCALE).astype(b16)
        return carry

    lax.fori_loop(0, q_ref.shape[2] // LANES, one_pair, 0, unroll=3)


def key_kernel(slots, begin, final, place, lengths, k_ref, v_ref, *refs):
    q_refs, g_refs, e_refs = refs[:slots], refs[slots : 2 * slots], refs[2 * slots : 3 * slots]
    refs = refs[3 * slots :]
    if not begin:
        dk_in, dv_in = refs[:2]
        refs = refs[2:]
    dk_ref, dv_ref = refs
    length = lengths[pl.program_id(0)]
    rows = k_ref.shape[1]
    lane = lane_iota(rows)
    dead = place[0] * rows + lax.broadcasted_iota(jnp.int32, (rows, LANES), 0) >= length
    mask = jnp.where((lane == MASK_LANE) & dead, MASKED, 0.0)
    minus = jnp.full((rows, LANES), -1.0, f32)

    def one_pair(pair, carry):
        cols = pair_columns(pair)
        levels = [(keep_lanes(minus, lane, 6 * pair + 3 * h) + mask).astype(b16) for h in range(2)]
        corrs = [
            keep_lanes(minus, lane, CORR_LANE + 6 * pair + 3 * h).astype(b16) for h in range(2)
        ]
        keys = jnp.concatenate([stack_heads(k_ref[0, :, cols]), jnp.concatenate(levels, 0)], 1)
        values = jnp.concatenate([stack_heads(v_ref[0, :, cols]), jnp.concatenate(corrs, 0)], 1)
        dkeys = jnp.zeros((2 * rows, LANES), f32)
        dvalues = jnp.zeros((2 * rows, LANES), f32)
        for s in range(slots):
            query, grad, extra = q_refs[s][0, :, cols], g_refs[s][0, :, cols], e_refs[s][0]
            weights = jnp.exp2(dot_nt(keys, jnp.concatenate([query, extra], 1)) * COEF)
            terms = dot_nt(values, jnp.concatenate([grad, extra], 1))
            dvalues = dvalues + dot_nn(weights.astype(b16), grad)
            dkeys = dkeys + dot_nn((weights * terms).astype(b16), query)
        dk, dv = join_heads(dkeys) * SCALE, join_heads(dvalues)
        if not begin:
            dk, dv = dk + dk_in[0, :, cols], dv + dv_in[0, :, cols]
        dk_ref[0, :, cols] = dk.astype(dk_ref.dtype)
        dv_ref[0, :, cols] = dv.astype(dv_ref.dtype)
        return carry

    lax.fori_loop(0, k_ref.shape[2] // LANES, one_pair, 0, unroll=3)


def third(block, width, which, seq_at=0):
    return pl.BlockSpec((1, block, width), lambda seq, *_: (seq_at + seq, 0, which))


def lanes_spec(block, at, seq_at=0):
    return pl.BlockSpec((1, block, LANES), lambda seq, *_: (seq_at + seq, 0, at))


def light():
    return pl.CostEstimate(flops=1000000, bytes_accessed=1000000, transcendentals=0)


def attend_forward(own, slots_qkv, bases, lengths, norms, state=(), final=False):
    slots = len(slots_qkv)
    seqs, block, triple = own.shape
    width = triple // 3
    q, k, v = (third(block, width, n) for n in range(3))
    part = jax.ShapeDtypeStruct((seqs, block, width), f32)
    if final:
        shapes = [part, jax.ShapeDtypeStruct((seqs, block, LANES), f32)]
        outs = [q, lanes_spec(block, 0)]
    else:
        shapes, outs = [part] * 3, [q] * 3
    return pl.pallas_call(
        functools.partial(forward_kernel, slots, not state, final),
        grid_spec=pltpu.PrefetchScalarGridSpec(
            num_scalar_prefetch=3,
            grid=(seqs,),
            in_specs=[q] + [k] * slots + [v] * slots + [q] * len(state),
            out_specs=outs,
            scratch_shapes=[pltpu.VMEM((slots, block, LANES), b16)],
        ),
        out_shape=shapes,
        compiler_params=pltpu.CompilerParams(vmem_limit_bytes=VMEM),
        cost_estimate=light(),
    )(bases, lengths, norms, own, *slots_qkv, *slots_qkv, *state)


def attend_query(seq_at, count, slots_qkv, grads, bases, lengths):
    slots = len(slots_qkv)
    block, triple = slots_qkv[0].shape[1:]
    width = triple // 3
    q, k, v = (third(block, width, n, seq_at) for n in range(3))
    return pl.pallas_call(
        functools.partial(query_kernel, slots),
        grid_spec=pltpu.PrefetchScalarGridSpec(
            num_scalar_prefetch=2,
            grid=(count,),
            in_specs=[q, q, lanes_spec(block, width // LANES, seq_at)]
            + [k] * slots
            + [v] * slots,
            out_specs=third(block, width, 0),
            scratch_shapes=[pltpu.VMEM((slots, block, LANES), b16)],
        ),
        out_shape=jax.ShapeDtypeStruct((count, block, width), b16),
        compiler_params=pltpu.CompilerParams(vmem_limit_bytes=VMEM_BACK),
        cost_estimate=light(),
    )(bases, lengths[seq_at : seq_at + count], slots_qkv[0], grads, grads, *slots_qkv, *slots_qkv)


def attend_keys(own, slots_qkv, slots_grads, place, lengths, state=(), final=False):
    slots = len(slots_qkv)
    seqs, block, triple = own.shape
    width = triple // 3
    q, k, v = (third(block, width, n) for n in range(3))
    shape = jax.ShapeDtypeStruct((seqs, block, width), b16 if final else f32)
    return pl.pallas_call(
        functools.partial(key_kernel, slots, not state, final),
        grid_spec=pltpu.PrefetchScalarGridSpec(
            num_scalar_prefetch=2,
            grid=(seqs,),
            in_specs=[k, v]
            + [q] * (2 * slots)
            + [lanes_spec(block, width // LANES)] * slots
            + [q] * len(state),
            out_specs=[q, q],
        ),
        out_shape=[shape, shape],
        compiler_params=pltpu.CompilerParams(vmem_limit_bytes=VMEM_BACK),
        cost_estimate=light(),
    )(place, lengths, own, own, *slots_qkv, *slots_grads, *slots_grads, *state)


def place_corr(dattended, attended, extra):
    rows, width = dattended.shape
    return pl.pallas_call(
        corr_kernel,
        out_shape=jax.ShapeDtypeStruct((rows, width + LANES), b16),
        compiler_params=pltpu.CompilerParams(vmem_limit_bytes=VMEM),
    )(dattended, attended, extra)


def layer_norm(value, gain, shift):
    mean = jnp.mean(value, axis=-1, keepdims=True)
    centred = value - mean
    spread = jnp.mean(centred * centred, axis=-1, keepdims=True)
    return centred * lax.rsqrt(spread + EPS) * gain + shift


def per_device(
    tokens,
    lengths,
    attend_weight,
    query_bias,
    value_bias,
    mixing_weight,
    mixing_bias,
    first_gain,
    first_shift,
    up_weight,
    up_bias,
    down_weight,
    down_bias,
    second_gain,
    second_shift,
    cotangent,
):
    seqs, block, width = tokens.shape
    rows = seqs * block
    owners = lax.axis_size("fsdp")
    blocks = lax.axis_size("ctx")
    place = lax.axis_index("ctx")
    share = width // owners
    steps = blocks // 2

    flat = tokens.reshape(rows, width)
    flat_low = flat.astype(b16)
    own_tokens = flat_low.reshape(seqs, block, width)
    own_tokens, attend_weight, mixing_weight = together(own_tokens, attend_weight, mixing_weight)

    spots = ring_slots("ctx")
    bases = spots * block

    def pick(blocks_at):
        keys = list(blocks_at)
        return keys, [blocks_at[k] for k in keys]

    def complete(got, near):
        blocks_at = dict(zip(keys, got))
        far = between({k: v for k, v in blocks_at.items() if k}, "fsdp")
        return blocks_at | far | {1: near}

    tr, tl = ring_step(own_tokens, own_tokens, "ctx")
    keys, attend_got = pick(across(attend_weight, "fsdp"))
    small = jnp.concatenate(
        [query_bias, value_bias, mixing_bias, first_gain, first_shift, down_bias,
         second_gain, second_shift, up_bias]
    )
    small_rows = -(-small.shape[0] // (16 * LANES)) * 16
    small = jnp.pad(small, (0, small_rows * LANES - small.shape[0])).reshape(small_rows, LANES)
    _, small_got = pick(across(small, "fsdp"))
    attend_near = between({0: attend_weight}, "fsdp")[1]
    tr, tl, mixing_weight, up_weight, attend_near, *got = together(
        tr, tl, mixing_weight, up_weight, attend_near, *attend_got, *small_got
    )
    attend_got, small_got = got[: len(keys)], got[len(keys) :]
    token_slots = [own_tokens, tr, tl]

    tr, tl = ring_step(tr, tl, "ctx")
    attend_blocks = complete(attend_got, attend_near)
    _, mixing_got = pick(across(mixing_weight, "fsdp"))
    _, up_got = pick(across(up_weight, "fsdp"))
    small_blocks = dict(zip(keys, small_got))
    small_full = in_order(small_blocks | between(small_blocks, "fsdp"), "fsdp")
    small_full = small_full.reshape(owners, -1).astype(f32)
    vectors = small_full[:, : 8 * share].reshape(owners, 8, share).transpose(1, 0, 2)
    vectors = vectors.reshape(8, width)
    qbias, vbias, mixbias, fgain, fshift, downbias, sgain, sshift = (
        vectors[k : k + 1] for k in range(8)
    )
    upbias = small_full[:, 8 * share : 8 * share + up_bias.shape[0]].reshape(1, -1)
    bias = jnp.concatenate([qbias, jnp.zeros_like(qbias), vbias], 1)
    attend_full = in_order(attend_blocks, "fsdp")
    slots_qkv, norms = project(token_slots, attend_full, bias)
    mixing_near = between({0: mixing_weight}, "fsdp")[1]
    up_near = between({0: up_weight}, "fsdp")[1]
    tr, tl, down_weight, mixing_near, up_near, *rest = together(
        tr, tl, down_weight, mixing_near, up_near, *mixing_got, *slots_qkv
    )
    mixing_got, slots_qkv = rest[: len(keys)], rest[len(keys) :]
    token_slots += [tr, tl]

    state = ()
    used = 0
    for step in range(3, steps + 1):
        last = step == steps
        nr, nl = ring_last(tr, tl, "ctx") if last else ring_step(tr, tl, "ctx")
        fresh, more = project(token_slots[len(slots_qkv) :], attend_full, bias)
        slots_qkv += fresh
        norms = jnp.maximum(norms, more)
        if step == 3:
            _, down_got = pick(across(down_weight, "fsdp"))
            down_near = between({0: down_weight}, "fsdp")[1]
            mixing_full = in_order(complete(mixing_got, mixing_near), "fsdp")
        if last:
            up_blocks = complete(up_got, up_near)
            tr, tl, *slots_qkv = together(nr, nl, *slots_qkv)
            token_slots.append(jnp.concatenate([tr, tl], 0))
        else:
            use = slice(used, len(slots_qkv))
            state = attend_forward(
                slots_qkv[0], slots_qkv[use], bases[use], lengths, norms, tuple(state)
            )
            used = len(slots_qkv)
            tr, tl, mixing_full, *rest = together(nr, nl, mixing_full, *up_got, *state)
            up_got, state = rest[: len(keys)], rest[len(keys) :]
            token_slots += [tr, tl]
    fresh, more = project(token_slots[len(slots_qkv) :], attend_full, bias)
    slots_qkv += fresh
    norms = jnp.maximum(norms, more)
    attended3, extra = attend_forward(
        slots_qkv[0], slots_qkv[used:], bases[used:], lengths, norms, tuple(state), True
    )
    up_full = in_order(up_blocks, "fsdp")
    down_full = in_order(complete(down_got, down_near), "fsdp")

    attended = attended3.reshape(rows, width)
    attended_low = attended.astype(b16)
    mixed = jnp.dot(attended_low, mixing_full, preferred_element_type=f32) + mixbias
    hidden = flat + mixed
    first, first_back = jax.vjp(layer_norm, hidden, fgain, fshift)
    first_low = first.astype(b16)
    act_low, slope, branch = feed_forward(first_low, up_full, upbias, down_full)
    summed = first + branch + downbias
    result, second_back = jax.vjp(layer_norm, summed, sgain, sshift)
    dsummed, grad_sgain, grad_sshift = second_back(cotangent.reshape(rows, width))
    dbranch = dsummed.astype(b16)
    grad_down = jnp.einsum("rf,rd->fd", act_low, dbranch, preferred_element_type=f32).astype(b16)
    down_send, down_keep = core_parts(grad_down.reshape(owners, -1, width))
    down_got = swap(down_send, "fsdp", 1)
    dpre, grad_upbias, dfirst = feed_backward(dbranch, down_full, slope, up_full, dsummed)
    dpre, dfirst, down_got = together(dpre, dfirst, down_got)
    grad_up = jnp.einsum("rd,rf->df", first_low, dpre, preferred_element_type=f32).astype(b16)
    up_send, up_keep = core_parts(grad_up.reshape(owners, share, -1))
    up_got = swap(up_send, "fsdp", 1)
    way_down, end_down = chip_sum(added(down_keep, down_got))
    dhidden, grad_fgain, grad_fshift = first_back(dfirst)
    dmixed = dhidden.astype(b16)
    dattended = jnp.einsum("re,de->rd", dmixed, mixing_full, preferred_element_type=f32)

    grads = place_corr(dattended, attended, extra.reshape(rows, LANES))
    grads = grads.reshape(seqs, block, width + LANES)
    grads, attended_low, dmixed, up_got = together(grads, attended_low, dmixed, up_got)

    def summed_rows(x):
        return jnp.sum(x.astype(f32), axis=0, keepdims=True)

    steps_ctx = block_sum_steps(blocks, 0)
    place1 = place.reshape(1)

    gr, gl = ring_step(grads, grads, "ctx")
    way_up, end_up = chip_sum(added(up_keep, up_got))
    dquery = [attend_query(0, 1, slots_qkv, grads, bases, lengths)]
    gr, gl, grads, dquery[0], dmixed, *way_down = together(
        gr, gl, grads, dquery[0], dmixed, *way_down
    )
    grad_slots = [grads, gr, gl]

    gr, gl = ring_step(gr, gl, "ctx")
    way_down, end_down = steps_ctx[0](end_down(*way_down))
    grad_mixing = jnp.einsum("rd,re->de", attended_low, dmixed, preferred_element_type=f32)
    dquery.append(attend_query(1, 1, slots_qkv, grads, bases, lengths))
    gr, gl, grad_mixing, dquery[1], *ways = together(
        gr, gl, grad_mixing, dquery[1], *way_down, *way_up
    )
    way_down, way_up = ways[:2], ways[2:]
    grad_slots += [gr, gl]
    dquery = jnp.concatenate(dquery, 0).reshape(rows, width)

    vectors = jnp.concatenate(
        [summed_rows(dmixed), grad_fgain, grad_fshift, summed_rows(dbranch), grad_sgain,
         grad_sshift, summed_rows(dquery)],
        0,
    )
    count = vectors.shape[0]
    (vectors,) = together(vectors.astype(b16).reshape(count, owners, share).transpose(1, 0, 2))
    vectors = jnp.pad(vectors, ((0, 0), (0, 0), (0, width - share)))
    wide = grad_upbias.astype(b16).reshape(owners, 1, -1)
    wide = jnp.pad(wide, ((0, 0), (0, 0), (0, width - wide.shape[2])))
    need = count + 1 + row_pad(2 * share + count + 1, blocks)
    tail = jnp.zeros((owners, need - count - 1, width), f32)
    (vectors,) = together(jnp.concatenate([vectors, wide], 1).astype(b16))
    vectors = jnp.concatenate([vectors, tail.astype(b16)], 1)
    dkv = ()
    used = 0
    for step in range(3, steps + 1):
        last = step == steps
        nr, nl = ring_last(gr, gl, "ctx") if last else ring_step(gr, gl, "ctx")
        if step == 3:
            grad_query = jnp.einsum("rd,re->de", flat_low, dquery, preferred_element_type=f32)
            mixed_parts = jnp.concatenate(
                [
                    grad_mixing.astype(b16).reshape(owners, share, width),
                    grad_query.astype(b16).reshape(owners, share, width),
                    vectors,
                ],
                1,
            )
            third_send, third_keep = core_parts(mixed_parts)
            third_got = swap(third_send, "fsdp", 1)
            way_down, end_down = steps_ctx[1](end_down(*way_down))
            way_up, end_up = steps_ctx[0](end_up(*way_up))
        if last:
            way_third, end_third = chip_sum(added(third_keep, third_got))
            way_down, end_down = steps_ctx[2](end_down(*way_down))
            way_up, end_up = steps_ctx[1](end_up(*way_up))
        use = slice(used, len(grad_slots) - (0 if last else 2))
        dkv = attend_keys(
            slots_qkv[0], slots_qkv[use], grad_slots[use], place1, lengths, tuple(dkv)
        )
        used = use.stop
        gr, gl, dkv0, dkv1, third_got, *ways = together(
            nr, nl, *dkv, third_got, *way_down, *way_up
        )
        way_down, way_up = ways[:2], ways[2:]
        dkv = (dkv0, dkv1)
        grad_slots += [jnp.concatenate([gr, gl], 0)] if last else [gr, gl]

    way_down, end_down = steps_ctx[3](end_down(*way_down))
    way_up, end_up = steps_ctx[2](end_up(*way_up))
    dkeys, dvalues = attend_keys(
        slots_qkv[0], slots_qkv[used:], grad_slots[used:], place1, lengths, tuple(dkv), True
    )
    dkeys, dvalues, *ways = together(dkeys, dvalues, *way_down, *way_up, *way_third)
    way_down, way_up, way_third = ways[:2], ways[2:4], ways[4:]
    dkeys, dvalues = dkeys.reshape(rows, width), dvalues.reshape(rows, width)
    dlate = jnp.concatenate([dkeys, dvalues], 1)
    tokens_across = flat_low.T

    core = lax.axis_index("fsdp") % 2
    first_column = (jnp.arange(LANES) == 0).astype(b16)
    bias_columns = jnp.broadcast_to(first_column, (rows, LANES))
    vector = jnp.einsum("rd,re->de", dvalues, bias_columns, preferred_element_type=f32)
    vector = vector.reshape(owners // 2, 2, share, LANES)

    def late_part(which):
        mine = lax.dynamic_index_in_dim(
            tokens_across.reshape(owners // 2, 2, share, rows), which, 1, keepdims=False
        )
        main = jnp.einsum("osr,re->ose", mine, dlate, preferred_element_type=f32)
        extra_columns = lax.dynamic_index_in_dim(vector, which, 1, keepdims=False)
        return jnp.concatenate([main, extra_columns], 2).astype(b16)

    late_got = swap(late_part(1 - core), "fsdp", 1)
    late_keep = late_part(core)
    dprojected = jnp.concatenate([dquery, dlate], 1)

    tokens_grad = dhidden + jnp.einsum(
        "re,de->rd", dprojected, attend_full, preferred_element_type=f32
    )

    chains = [
        (way_down, end_down, steps_ctx[4:]),
        (way_up, end_up, steps_ctx[3:]),
        (way_third, end_third, steps_ctx),
        ((late_keep, late_got), added, [chip_sum] + block_sum_steps(blocks, 1)),
    ]
    sums = [None] * len(chains)
    begin = True
    while any(chains):
        active = [k for k, chain in enumerate(chains) if chain]
        for k in active:
            way, end, left = chains[k]
            if begin and k == 3:
                continue
            value = end(*way)
            if left:
                chains[k] = (*left[0](value), left[1:])
            else:
                sums[k], chains[k] = value, None
        active = [k for k, chain in enumerate(chains) if chain]
        ways = [tuple(chains[k][0]) for k in active]
        if begin:
            ways, tokens_grad = together(ways, tokens_grad)
        elif active:
            (ways,) = together(ways)
        for k, way in zip(active, ways):
            chains[k] = (way,) + chains[k][1:]
        begin = False
    one, two, three, four = (v.astype(f32) for v in sums)

    own_down = one[: down_weight.shape[0]]
    own_up = two[:share]
    own_mixing = three[:share]
    own_attend = jnp.concatenate([three[share : 2 * share], four[:share, : 2 * width]], 1)
    own_vbias = four[:share, 2 * width]
    at = 2 * share
    (
        own_mixbias, own_fgain, own_fshift, own_downbias, own_sgain, own_sshift, own_qbias,
    ) = (three[at + k, :share] for k in range(count))
    own_upbias = three[at + count, : up_bias.shape[0]]
    return (
        result.reshape(seqs, block, width),
        tokens_grad.reshape(seqs, block, width),
        own_attend,
        own_qbias,
        own_vbias,
        own_mixing,
        own_mixbias,
        own_fgain,
        own_fshift,
        own_up,
        own_upbias,
        own_down,
        own_downbias,
        own_sgain,
        own_sshift,
    )


def solution(mesh):
    rows = P("fsdp", "ctx", None)
    matrix = P("fsdp", None)
    vector = P("fsdp")
    return jax.shard_map(
        per_device,
        mesh=mesh,
        in_specs=(
            rows, vector, matrix, vector, vector, matrix, vector, vector, vector,
            matrix, vector, matrix, vector, vector, vector, rows,
        ),
        out_specs=(
            rows, rows, matrix, vector, vector, matrix, vector, vector, vector,
            matrix, vector, matrix, vector, vector, vector,
        ),
        check_vma=False,
    )
```
